512 devices in a mesh: view: 16 (over z), head: 32 (over y, x, core).
Axes of the slice: x: 4, y: 4, z: 16, core: 2. Of those that a mesh axis runs over, the one named last changes fastest.
Arguments:
- queries: bfloat16 [32768, 4096], P('view', 'head'), may hold values from -6 to 6
- key_tokens: bfloat16 [32768, 4096], P('view', 'head'), may hold values from -6 to 6
- value_tokens: bfloat16 [32768, 4096], P('view', 'head'), may hold values from -64 to 64
- block_lists: int32 [512, 4], P('view'), may hold values from -1 to 479, as said below
- gain_soft: float32 [4096], P('head'), may hold values from 0.25 to 1.75
- gain_linear: float32 [4096], P('head'), may hold values from 0.25 to 1.75
Outputs:
- layer_out: bfloat16 [32768, 4096], P('view', 'head')
The draws below stay inside these ranges and needn't reach their ends.
Inputs may be any that keep to these rules, and one draw needn't show every extreme that they name: `block_lists`: rows of the first view are all -1. Each row of a later view v lists 4 distinct blocks, all in views before v; the rows of view v together list exactly 4 distinct blocks of each earlier view.
All inputs are finite; a program needn't handle non-finite values.
Results may differ from the reference program's by a relative error of at most 0.0038.
Values may be sent and summed in bfloat16 or wider, within the bound.
A program may use at most 64 MiB of HBM per device.

```python
import jax
import jax.numpy as jnp
from jax import lax

HEAD_DIM = 128
TOK_VIEW = 2048
BLOCK = 64
TOPK = 4
CAP = 4
HEADS = 32
VIEWS = 16
QB_VIEW = 32
QBLOCKS = 512
TOKENS = 32768


def draw_queries(key, part):
    own_key = jax.random.fold_in(key, 3)
    result = jnp.clip(jax.random.normal(own_key, (TOKENS, HEADS * HEAD_DIM)), -6.0, 6.0)
    return result.astype(jnp.bfloat16)


def draw_key_tokens(key, part):
    own_key = jax.random.fold_in(key, 4)
    result = jnp.clip(jax.random.normal(own_key, (TOKENS, HEADS * HEAD_DIM)), -6.0, 6.0)
    return result.astype(jnp.bfloat16)


def draw_value_tokens(key, part):
    key = jax.random.fold_in(key, 5)
    key_head = jax.random.fold_in(key, 0)
    key_main = jax.random.fold_in(key, 2)
    head_index = jnp.arange(HEADS).astype(jnp.float32) / (HEADS - 1)
    jitter = jnp.exp(jax.random.uniform(key_head, (HEADS,), minval=-0.2, maxval=0.2))
    factor = 3.0 ** head_index * jitter
    main = jnp.clip(jax.random.normal(key_main, (TOKENS, HEADS * HEAD_DIM)), -4.0, 4.0)
    column_scale = jnp.repeat(factor, HEAD_DIM)
    return (main * column_scale[None, :]).astype(jnp.bfloat16)


def draw_block_lists(key, part):
    key = jax.random.fold_in(key, 7)
    key_perm, key_score, key_shift = jax.random.split(key, 3)
    perm_keys = jax.random.split(key_perm, VIEWS * VIEWS)
    orderings = jax.vmap(lambda sub_key: jax.random.permutation(sub_key, QB_VIEW))(perm_keys)
    orderings = orderings.reshape(VIEWS, VIEWS, QB_VIEW).astype(jnp.int32)
    owners = jnp.arange(VIEWS, dtype=jnp.int32)
    last_pair = (owners[:, None] == VIEWS - 1) & (owners[None, :] == VIEWS - 2)
    offset = jnp.where(last_pair, QB_VIEW - 1 - orderings[:, :, 0], 0)
    orderings = ((orderings + offset[:, :, None]) % QB_VIEW)[:, :, :CAP].astype(jnp.int32)
    pooled_ids = owners[None, :, None] * QB_VIEW + orderings
    usable = jnp.broadcast_to(owners[None, :, None] < owners[:, None, None], (VIEWS, VIEWS, CAP)).reshape(VIEWS, VIEWS * CAP)
    scores = jax.random.randint(key_score, (VIEWS, VIEWS * CAP), 0, 1 << 16) * (VIEWS * CAP) + jnp.arange(VIEWS * CAP, dtype=jnp.int32)[None, :]
    scores = jnp.where(usable, scores, scores + (1 << 28))
    ordering = jnp.argsort(scores, axis=1)
    pooled = jnp.take_along_axis(pooled_ids.reshape(VIEWS, VIEWS * CAP), ordering, axis=1)
    live_count = owners * CAP
    rotation = jax.random.randint(key_shift, (VIEWS,), 0, 1 << 16)
    steps_in = jnp.arange(QB_VIEW, dtype=jnp.int32)[:, None] * TOPK + jnp.arange(TOPK, dtype=jnp.int32)[None, :]
    positions = (steps_in[None, :, :] + rotation[:, None, None]) % jnp.maximum(live_count, 1)[:, None, None]
    picked = jnp.take_along_axis(pooled, positions.reshape(VIEWS, QB_VIEW * TOPK), axis=1).reshape(VIEWS, QB_VIEW, TOPK)
    picked = jnp.where(live_count[:, None, None] > 0, picked, -1)
    return picked.reshape(VIEWS * QB_VIEW, TOPK).astype(jnp.int32)


def setup_inputs(seed: int = 0) -> dict:
    keys = jax.random.split(jax.random.key(seed), 7)
    queries = draw_queries(jax.random.fold_in(keys[6], 71), 0)
    key_tokens = draw_key_tokens(jax.random.fold_in(keys[6], 71), 0)
    value_tokens = draw_value_tokens(jax.random.fold_in(keys[6], 71), 0)
    block_lists = draw_block_lists(jax.random.fold_in(keys[6], 71), 0)
    gain_soft = jnp.clip(1.0 + 0.15 * jax.random.normal(keys[4], (HEADS * HEAD_DIM,), jnp.float32), 0.25, 1.75)
    gain_linear = jnp.clip(1.0 + 0.15 * jax.random.normal(keys[5], (HEADS * HEAD_DIM,), jnp.float32), 0.25, 1.75)
    return dict(queries=queries, key_tokens=key_tokens, value_tokens=value_tokens, block_lists=block_lists, gain_soft=gain_soft, gain_linear=gain_linear)


norm_eps = 1e-06

def feature(values_in):
    return jax.nn.elu(values_in) + 1.0

def reference(queries, key_tokens, value_tokens, block_lists, gain_soft, gain_linear):
    score_scale = HEAD_DIM ** (-0.5)
    query_heads = queries.reshape(VIEWS, TOK_VIEW, HEADS, HEAD_DIM).transpose(2, 0, 1, 3)
    key_heads = key_tokens.reshape(VIEWS, TOK_VIEW, HEADS, HEAD_DIM).transpose(2, 0, 1, 3)
    value_heads = value_tokens.reshape(VIEWS, TOK_VIEW, HEADS, HEAD_DIM).transpose(2, 0, 1, 3)
    key_blocks = key_tokens.reshape(QBLOCKS, BLOCK, HEADS, HEAD_DIM).transpose(2, 0, 1, 3)
    value_blocks = value_tokens.reshape(QBLOCKS, BLOCK, HEADS, HEAD_DIM).transpose(2, 0, 1, 3)
    lists_view = block_lists.reshape(VIEWS, QB_VIEW, TOPK)
    causal = jnp.arange(TOK_VIEW)[:, None] >= jnp.arange(TOK_VIEW)[None, :]

    def per_head(head_inputs):
        query_h, key_h, value_h, kblock_h, vblock_h = head_inputs
        states = jnp.einsum('vtd,vte->vde', feature(key_h.astype(jnp.float32)), value_h.astype(jnp.float32), precision=lax.Precision.HIGHEST)
        running = jnp.cumsum(states, axis=0)
        prefix = jnp.concatenate([jnp.zeros((1, HEAD_DIM, HEAD_DIM), jnp.float32), running[:-1]], axis=0)

        def per_view(view_inputs):
            query_v, key_v, value_v, prefix_v, lists_v = view_inputs
            listed = lists_v >= 0
            position = jnp.maximum(lists_v, 0).astype(jnp.int32)
            remote_keys = jnp.take(kblock_h, position, axis=0).reshape(QB_VIEW, TOPK * BLOCK, HEAD_DIM).astype(jnp.float32)
            remote_values = jnp.take(vblock_h, position, axis=0).reshape(QB_VIEW, TOPK * BLOCK, HEAD_DIM).astype(jnp.float32)
            remote_mask = jnp.repeat(listed, BLOCK, axis=1)
            query_f = query_v.astype(jnp.float32)
            local_scores = jnp.einsum('rd,td->rt', query_f, key_v.astype(jnp.float32)) * score_scale
            local_scores = jnp.where(causal, local_scores, -jnp.inf)
            query_blocks = query_f.reshape(QB_VIEW, BLOCK, HEAD_DIM)
            remote_scores = jnp.einsum('nbd,nkd->nbk', query_blocks, remote_keys) * score_scale
            remote_scores = jnp.where(remote_mask[:, None, :], remote_scores, -jnp.inf)
            row_max = jnp.maximum(lax.optimization_barrier(jnp.max(local_scores, axis=1)), lax.optimization_barrier(jnp.max(remote_scores, axis=2)).reshape(TOK_VIEW))
            local_probs = jnp.exp(local_scores - row_max[:, None])
            remote_probs = jnp.exp(remote_scores - row_max.reshape(QB_VIEW, BLOCK)[:, :, None])
            row_total = lax.optimization_barrier(jnp.sum(local_probs, axis=1)) + lax.optimization_barrier(jnp.sum(remote_probs, axis=2)).reshape(TOK_VIEW)
            local_weights = lax.optimization_barrier(local_probs.astype(jnp.bfloat16)).astype(jnp.float32)
            remote_weights = lax.optimization_barrier(remote_probs.astype(jnp.bfloat16)).astype(jnp.float32)
            weighted = jnp.einsum('rt,td->rd', local_weights, value_v.astype(jnp.float32))
            weighted = weighted + jnp.einsum('nbk,nkd->nbd', remote_weights, remote_values).reshape(TOK_VIEW, HEAD_DIM)
            attended = weighted / row_total[:, None]
            query_feat = feature(query_f)
            linear = jnp.dot(query_feat, prefix_v, precision=lax.Precision.HIGHEST)
            weight = jnp.einsum('nbd,nkd->nbk', query_feat.reshape(QB_VIEW, BLOCK, HEAD_DIM), feature(remote_keys), precision=lax.Precision.HIGHEST)
            weight = weight * remote_mask[:, None, :].astype(jnp.float32)
            correction = jnp.einsum('nbk,nkd->nbd', weight, remote_values, precision=lax.Precision.HIGHEST).reshape(TOK_VIEW, HEAD_DIM)
            return (attended, linear - correction)
        return lax.map(per_view, (query_h, key_h, value_h, prefix, lists_view))
    attended, linear = lax.map(per_head, (query_heads, key_heads, value_heads, key_blocks, value_blocks))
    attended = attended.transpose(1, 2, 0, 3).reshape(TOKENS, HEADS, HEAD_DIM)
    linear = linear.transpose(1, 2, 0, 3).reshape(TOKENS, HEADS, HEAD_DIM)
    soft_scale = lax.rsqrt(lax.optimization_barrier(jnp.mean(attended * attended, axis=(1, 2))) + norm_eps)
    linear_scale = lax.rsqrt(lax.optimization_barrier(jnp.mean(linear * linear, axis=(1, 2))) + norm_eps)
    layer_out = attended * soft_scale[:, None, None] * gain_soft.reshape(HEADS, HEAD_DIM) + linear * linear_scale[:, None, None] * gain_linear.reshape(HEADS, HEAD_DIM)
    return layer_out.reshape(TOKENS, HEADS * HEAD_DIM).astype(jnp.bfloat16)
```

```python
import functools

import jax
import jax.numpy as jnp
from jax import lax
from jax.experimental import pallas as pl
from jax.experimental.pallas import tpu as pltpu
from jax.sharding import PartitionSpec as P

HEAD_DIM = 128
BLOCK = 64
TOPK = 4
CAP = 4
EPS = 1e-06
SPLITS = (2, 4, 4)
MESH = pl.DeviceIdType.MESH
NT = (((1,), (1,)), ((), ()))
TN = (((0,), (0,)), ((), ()))
HIGHEST = lax.Precision.HIGHEST


def feature(x):
    return jnp.where(x > 0, x + 1.0, jnp.exp(jnp.minimum(x, 0.0)))


def matmul(a, b):
    return jnp.dot(a, b, preferred_element_type=jnp.float32)


def matmul_nt(a, b, precision=None):
    return lax.dot_general(a, b, NT, precision=precision, preferred_element_type=jnp.float32)


def matmul_tn(a, b, precision=None):
    return lax.dot_general(a, b, TN, precision=precision, preferred_element_type=jnp.float32)


def send_order(views):
    half = views // 2
    low, high = list(range(half, views)), []
    while low:
        high.append(low.pop())
        if low:
            high.append(low.pop(0))
    return high + list(range(half - 1, 0, -1))


def kernel(
    views, heads, splits, rows,
    q_ref, k_ref, v_ref, plan_ref, pos_ref, gain_s_ref, gain_l_ref, out_ref,
    plans, plan_smem, stage, recv, states, entering, leaving, own_state,
    acc, top, total, att, lin, sums, sums_in,
    plan_send, plan_recv, bulk_send, bulk_recv, chain_sem, local_sem, sum_send, sum_recv,
):
    me = lax.axis_index("view")
    head = lax.axis_index("head")
    scale2 = 1.4426950408889634 * HEAD_DIM ** (-0.5)
    qtile = min(256, rows)
    qblocks = rows // BLOCK

    phases = []
    stride = 1
    for size in splits:
        place = head // stride % size
        phases.append([head + ((place + t) % size - place) * stride for t in range(1, size)])
        stride *= size

    barrier = pltpu.get_barrier_semaphore()
    for d in range(1, views):
        pl.semaphore_signal(
            barrier, inc=1, device_id=((me + d) % views, head), device_id_type=MESH
        )
    for partners in phases:
        for other in partners:
            pl.semaphore_signal(barrier, inc=1, device_id=(me, other), device_id_type=MESH)
    pl.semaphore_wait(barrier, views - 1 + sum(len(p) for p in phases))

    def plan_copy(slot, to):
        return pltpu.make_async_remote_copy(
            src_ref=plan_ref.at[to],
            dst_ref=plans.at[slot],
            send_sem=plan_send.at[to],
            recv_sem=plan_recv.at[slot],
            device_id=(to, head),
            device_id_type=MESH,
        )

    for u in range(views - 1):
        @pl.when(u < me)
        def _():
            plan_copy(me, u).start()

    own_state[...] = matmul_tn(
        feature(k_ref[...].reshape(rows, HEAD_DIM).astype(jnp.float32)).astype(jnp.bfloat16),
        v_ref[...].reshape(rows, HEAD_DIM),
    )

    def chain_copy():
        return pltpu.make_async_remote_copy(
            src_ref=leaving,
            dst_ref=entering,
            send_sem=chain_sem.at[0],
            recv_sem=chain_sem.at[1],
            device_id=((me + 1) % views, head),
            device_id_type=MESH,
        )

    @pl.when(me == 0)
    def _():
        leaving[...] = own_state[...]
        chain_copy().start()

    for w in range(1, views):
        @pl.when(w > me)
        def _():
            plan_copy(w, w).wait_recv()

    smem_copy = pltpu.make_async_copy(plans, plan_smem, local_sem)
    smem_copy.start()
    smem_copy.wait()

    def bulk_copy(slot, to):
        return pltpu.make_async_remote_copy(
            src_ref=stage.at[pl.ds(to * CAP, CAP)],
            dst_ref=recv.at[pl.ds(slot * CAP, CAP)],
            send_sem=bulk_send.at[to],
            recv_sem=bulk_recv.at[slot],
            device_id=(to, head),
            device_id_type=MESH,
        )

    for w in send_order(views):
        @pl.when(w > me)
        def _():
            for s in range(CAP):
                block = plan_smem[w, 0, s]
                stage[w * CAP + s, 0] = k_ref[block]
                stage[w * CAP + s, 1] = v_ref[block]
            bulk_copy(me, w).start()

    @pl.when(me > 0)
    def _():
        chain_copy().wait_recv()

        @pl.when(me < views - 1)
        def _():
            leaving[...] = entering[...] + own_state[...]
            chain_copy().start()

    row = lax.broadcasted_iota(jnp.int32, (qtile, qtile), 0)
    col = lax.broadcasted_iota(jnp.int32, (qtile, qtile), 1)

    per_tile = qtile // BLOCK

    def tile_of(ref, j):
        return ref[pl.ds(j * per_tile, per_tile)].reshape(qtile, HEAD_DIM)

    @pl.loop(0, rows // qtile)
    def _(i):
        mine = pl.ds(pl.multiple_of(i * qtile, qtile), qtile)
        q = q_ref[mine, :]
        s = jnp.where(row >= col, matmul_nt(q, tile_of(k_ref, i)), -jnp.inf)
        m = jnp.max(s, axis=1, keepdims=True)
        p = jnp.exp2((s - m) * scale2)
        l = jnp.sum(p, axis=1, keepdims=True)
        o = matmul(p.astype(jnp.bfloat16), tile_of(v_ref, i))

        def step(j, carry):
            m, l, o = carry
            s = matmul_nt(q, tile_of(k_ref, j))
            new = jnp.maximum(m, jnp.max(s, axis=1, keepdims=True))
            p = jnp.exp2((s - new) * scale2)
            fade = jnp.exp2((m - new) * scale2)
            l = l * fade + jnp.sum(p, axis=1, keepdims=True)
            o = o * fade + matmul(p.astype(jnp.bfloat16), tile_of(v_ref, j))
            return new, l, o

        m, l, o = lax.fori_loop(0, i, step, (m, l, o))
        acc[mine, :] = o
        top[mine, :] = jnp.broadcast_to(m, (qtile, HEAD_DIM))
        total[mine, :] = jnp.broadcast_to(l, (qtile, HEAD_DIM))

    @pl.loop(0, me)
    def _(u):
        bulk_copy(u, u).wait_recv()
        for s in range(CAP):
            states[u * CAP + s] = matmul_tn(
                feature(recv[u * CAP + s, 0].astype(jnp.float32)).astype(jnp.bfloat16),
                recv[u * CAP + s, 1],
            )

    @pl.when(me == 0)
    def _():
        att[...] = acc[...] / total[...]
        lin[...] = jnp.zeros_like(lin)

    @pl.when(me > 0)
    def _():
        @pl.loop(0, qblocks)
        def _(r):
            mine = pl.ds(pl.multiple_of(r * BLOCK, BLOCK), BLOCK)
            q = q_ref[mine, :]
            scores, values = [], []
            remaining = entering[...]
            for c in range(TOPK):
                at = pos_ref[r * TOPK + c]
                scores.append(matmul_nt(q, recv[at, 0]))
                values.append(recv[at, 1])
                remaining = remaining - states[at]
            s = jnp.concatenate(scores, axis=1)
            m_old = top[mine, :][:, :1]
            m = jnp.maximum(m_old, jnp.max(s, axis=1, keepdims=True))
            p = jnp.exp2((s - m) * scale2)
            fade = jnp.exp2((m_old - m) * scale2)
            l = total[mine, :][:, :1] * fade + jnp.sum(p, axis=1, keepdims=True)
            o = acc[mine, :] * fade + matmul(
                p.astype(jnp.bfloat16), jnp.concatenate(values, axis=0)
            )
            att[mine, :] = o / l
            qf = feature(q.astype(jnp.float32)).astype(jnp.bfloat16)
            coarse = remaining.astype(jnp.bfloat16)
            fine = (remaining - coarse.astype(jnp.float32)).astype(jnp.bfloat16)
            lin[mine, :] = matmul(qf, coarse) + matmul(qf, fine)

    parts = 4
    seg = rows // parts
    sub = lax.broadcasted_iota(jnp.int32, (2 * parts, HEAD_DIM), 0)

    def pick(i):
        return jnp.where(sub == i, 1.0, 0.0).astype(jnp.float32)

    partial = jnp.zeros((2 * parts, seg), jnp.float32)
    for t in range(parts):
        a = att[t * seg : (t + 1) * seg, :]
        b = lin[t * seg : (t + 1) * seg, :]
        partial = partial + matmul_nt(pick(2 * t), a * a, HIGHEST)
        partial = partial + matmul_nt(pick(2 * t + 1), b * b, HIGHEST)

    count = 0
    copies = []
    for phase, partners in enumerate(phases):
        sums[phase] = partial
        here = []
        for other in partners:
            copy = pltpu.make_async_remote_copy(
                src_ref=sums.at[phase],
                dst_ref=sums_in.at[count],
                send_sem=sum_send.at[count],
                recv_sem=sum_recv.at[count],
                device_id=(me, other),
                device_id_type=MESH,
            )
            copy.start()
            here.append((copy, count))
            count += 1
        for copy, at in here:
            copy.wait_recv()
            partial = partial + sums_in[at]
        copies += [copy for copy, _ in here]

    scales = lax.rsqrt(partial / (heads * HEAD_DIM) + EPS)
    gain_s, gain_l = gain_s_ref[...], gain_l_ref[...]
    for t in range(parts):
        span = slice(t * seg, (t + 1) * seg)
        soft = matmul_tn(scales, pick(2 * t), HIGHEST)
        linear = matmul_tn(scales, pick(2 * t + 1), HIGHEST)
        out_ref[span, :] = (
            att[span, :] * soft * gain_s + lin[span, :] * linear * gain_l
        ).astype(jnp.bfloat16)

    for copy in copies:
        copy.wait_send()
    for u in range(views - 1):
        @pl.when(u < me)
        def _():
            plan_copy(me, u).wait_send()
    for w in range(1, views):
        @pl.when(w > me)
        def _():
            bulk_copy(me, w).wait_send()

    @pl.when(me < views - 1)
    def _():
        chain_copy().wait_send()


def shards(views, heads, splits, q, k, v, lists, gain_s, gain_l):
    rows = q.shape[0]
    per_view = rows // BLOCK
    blocks = views * per_view
    flat = lists.reshape(-1)
    ids = jnp.arange(blocks, dtype=jnp.int32)
    present = jnp.any(flat[:, None] == ids[None, :], axis=0)
    table = present.reshape(views, per_view)
    within = jnp.arange(per_view, dtype=jnp.int32)
    earlier = within[None, :] < within[:, None]
    rank = jnp.sum(table[:, None, :] & earlier[None], axis=2, dtype=jnp.int32)
    slots = jnp.arange(HEAD_DIM, dtype=jnp.int32)
    chosen = table[:, None, :] & (rank[:, None, :] == slots[None, :, None])
    plan = jnp.sum(jnp.where(chosen, within[None, None, :], 0), axis=2, dtype=jnp.int32)
    place = (jnp.arange(views, dtype=jnp.int32)[:, None] * CAP + rank).reshape(-1)
    pos = jnp.sum(jnp.where(flat[:, None] == ids[None, :], place[None, :], 0), axis=1)

    phases = len(splits)
    partners = sum(s - 1 for s in splits)
    f32, bf16 = jnp.float32, jnp.bfloat16
    vmem = pl.BlockSpec(memory_space=pltpu.VMEM)
    smem = pl.BlockSpec(memory_space=pltpu.SMEM)
    dma = pltpu.SemaphoreType.DMA
    sums = (8, rows // 4)
    return pl.pallas_call(
        functools.partial(kernel, views, heads, splits, rows),
        out_shape=jax.ShapeDtypeStruct(q.shape, bf16),
        in_specs=[vmem, vmem, vmem, vmem, smem, vmem, vmem],
        out_specs=vmem,
        scratch_shapes=[
            pltpu.VMEM((views, 1, HEAD_DIM), jnp.int32),
            pltpu.SMEM((views, 1, HEAD_DIM), jnp.int32),
            pltpu.VMEM((views * CAP, 2, BLOCK, HEAD_DIM), bf16),
            pltpu.VMEM((views * CAP, 2, BLOCK, HEAD_DIM), bf16),
            pltpu.VMEM((views * CAP, HEAD_DIM, HEAD_DIM), f32),
            pltpu.VMEM((HEAD_DIM, HEAD_DIM), f32),
            pltpu.VMEM((HEAD_DIM, HEAD_DIM), f32),
            pltpu.VMEM((HEAD_DIM, HEAD_DIM), f32),
            pltpu.VMEM((rows, HEAD_DIM), f32),
            pltpu.VMEM((rows, HEAD_DIM), f32),
            pltpu.VMEM((rows, HEAD_DIM), f32),
            pltpu.VMEM((rows, HEAD_DIM), f32),
            pltpu.VMEM((rows, HEAD_DIM), f32),
            pltpu.VMEM((phases,) + sums, f32),
            pltpu.VMEM((partners,) + sums, f32),
            dma((views,)),
            dma((views,)),
            dma((views,)),
            dma((views,)),
            dma((2,)),
            dma,
            dma((partners,)),
            dma((partners,)),
        ],
        compiler_params=pltpu.CompilerParams(
            collective_id=0, has_side_effects=True, vmem_limit_bytes=48 * 1024 * 1024
        ),
    )(
        q,
        k.reshape(per_view, BLOCK, HEAD_DIM),
        v.reshape(per_view, BLOCK, HEAD_DIM),
        plan.reshape(views, 1, HEAD_DIM),
        pos,
        gain_s[None],
        gain_l[None],
    )


def solution(mesh, splits=SPLITS):
    views, heads = mesh.shape["view"], mesh.shape["head"]
    in_specs = (
        P("view", "head"),
        P("view", "head"),
        P("view", "head"),
        P("view", None),
        P("head"),
        P("head"),
    )
    return jax.shard_map(
        functools.partial(shards, views, heads, splits),
        mesh=mesh,
        in_specs=in_specs,
        out_specs=P("view", "head"),
        check_vma=False,
    )
```

```python
import functools

import jax
import jax.numpy as jnp
from jax import lax
from jax.experimental import pallas as pl
from jax.experimental.pallas import tpu as pltpu
from jax.sharding import PartitionSpec as P

HEAD_DIM = 128
BLOCK = 64
TOPK = 4
CAP = 4
EPS = 1e-06
SPLITS = (8, 4)
MESH = pl.DeviceIdType.MESH
NT = (((1,), (1,)), ((), ()))
TN = (((0,), (0,)), ((), ()))


def feature(x):
    return jnp.where(x > 0, x + 1.0, jnp.exp(jnp.minimum(x, 0.0)))


def matmul(a, b):
    return jnp.dot(a, b, preferred_element_type=jnp.float32)


def matmul_nt(a, b):
    return lax.dot_general(a, b, NT, preferred_element_type=jnp.float32)


def matmul_tn(a, b):
    return lax.dot_general(a, b, TN, preferred_element_type=jnp.float32)


def send_order(views):
    half = views // 2
    low, high = list(range(half, views)), []
    while low:
        high.append(low.pop())
        if low:
            high.append(low.pop(0))
    return high + list(range(half - 1, 0, -1))


def kernel(
    views, heads, splits, rows,
    q_hbm, k_hbm, v_hbm, plan_ref, pos_ref, gain_s_ref, gain_l_ref, out_ref,
    q_ref, k_ref, v_ref,
    plans, plan_smem, stage, recv, states, entering, leaving, own_state, members, earlier,
    acc, top, total, att, lin, sums, sums_in,
    plan_send, plan_recv, bulk_send, bulk_recv, member_send, member_recv,
    group_send, group_recv, local_sem, in_sem, sum_send, sum_recv,
):
    me = lax.axis_index("view")
    head = lax.axis_index("head")
    scale2 = 1.4426950408889634 * HEAD_DIM ** (-0.5)
    qtile = min(256, rows)
    group = 4 if views >= 16 else 2

    k_in = pltpu.make_async_copy(k_hbm, k_ref, in_sem.at[0])
    v_in = pltpu.make_async_copy(v_hbm, v_ref, in_sem.at[1])
    q_in = pltpu.make_async_copy(q_hbm, q_ref, in_sem.at[2])
    k_in.start()
    v_in.start()
    q_in.start()

    phases = []
    stride = 1
    for size in splits:
        place = head // stride % size
        phases.append([head + ((place + t) % size - place) * stride for t in range(1, size)])
        stride *= size

    barrier = pltpu.get_barrier_semaphore()
    for d in range(1, views):
        pl.semaphore_signal(
            barrier, inc=1, device_id=((me + d) % views, head), device_id_type=MESH
        )
    for partners in phases:
        for other in partners:
            pl.semaphore_signal(barrier, inc=1, device_id=(me, other), device_id_type=MESH)
    pl.semaphore_wait(barrier, views - 1 + sum(len(p) for p in phases))

    def plan_copy(slot, to):
        return pltpu.make_async_remote_copy(
            src_ref=plan_ref.at[to],
            dst_ref=plans.at[slot],
            send_sem=plan_send.at[to],
            recv_sem=plan_recv.at[slot],
            device_id=(to, head),
            device_id_type=MESH,
        )

    for u in range(views - 1):
        @pl.when(u < me)
        def _():
            plan_copy(me, u).start()

    k_in.wait()
    v_in.wait()
    own_state[...] = matmul_tn(
        feature(k_ref[...].reshape(rows, HEAD_DIM).astype(jnp.float32)).astype(jnp.bfloat16),
        v_ref[...].reshape(rows, HEAD_DIM),
    )
    leaving[0] = own_state[...].astype(jnp.bfloat16)
    member = me % group

    def member_copy(slot, step):
        return pltpu.make_async_remote_copy(
            src_ref=leaving.at[0],
            dst_ref=members.at[slot],
            send_sem=member_send.at[step],
            recv_sem=member_recv.at[slot],
            device_id=((me + step) % views, head),
            device_id_type=MESH,
        )

    for step in range(1, group):
        @pl.when(member + step < group)
        def _():
            member_copy(member, step).start()

    def group_copy(step):
        return pltpu.make_async_remote_copy(
            src_ref=leaving.at[1],
            dst_ref=earlier,
            send_sem=group_send.at[step - 1],
            recv_sem=group_recv,
            device_id=((me + step) % views, head),
            device_id_type=MESH,
        )

    def gather_prefix():
        entering[...] = jnp.zeros_like(entering)
        for slot in range(group - 1):
            @pl.when(slot < member)
            def _():
                member_copy(slot, 1).wait_recv()
                entering[...] += members[slot].astype(jnp.float32)

        @pl.when(me >= group)
        def _():
            group_copy(1).wait_recv()
            entering[...] += earlier[...].astype(jnp.float32)

    for w in range(1, views):
        @pl.when(w > me)
        def _():
            plan_copy(w, w).wait_recv()

    smem_copy = pltpu.make_async_copy(plans, plan_smem, local_sem)
    smem_copy.start()
    smem_copy.wait()

    @pl.when(member == group - 1)
    def _():
        gather_prefix()

        @pl.when(me < views - 1)
        def _():
            leaving[1] = (entering[...] + own_state[...]).astype(jnp.bfloat16)
            for step in range(1, group + 1):
                group_copy(step).start()

    def bulk_copy(slot, to):
        return pltpu.make_async_remote_copy(
            src_ref=stage.at[pl.ds(to * CAP, CAP)],
            dst_ref=recv.at[pl.ds(slot * CAP, CAP)],
            send_sem=bulk_send.at[to],
            recv_sem=bulk_recv.at[slot],
            device_id=(to, head),
            device_id_type=MESH,
        )

    for w in send_order(views):
        @pl.when(w > me)
        def _():
            for s in range(CAP):
                block = plan_smem[w, 0, s]
                stage[w * CAP + s, 0] = k_ref[block]
                stage[w * CAP + s, 1] = v_ref[block]
            bulk_copy(me, w).start()

    row = lax.broadcasted_iota(jnp.int32, (qtile, qtile), 0)
    col = lax.broadcasted_iota(jnp.int32, (qtile, qtile), 1)

    per_tile = qtile // BLOCK

    def tile_of(ref, j):
        return ref[pl.ds(j * per_tile, per_tile)].reshape(qtile, HEAD_DIM)

    q_in.wait()

    @pl.loop(0, rows // qtile)
    def _(i):
        mine = pl.ds(pl.multiple_of(i * qtile, qtile), qtile)
        q = q_ref[mine, :]
        s = jnp.where(row >= col, matmul_nt(q, tile_of(k_ref, i)), -jnp.inf)
        m = jnp.max(s, axis=1, keepdims=True)
        p = jnp.exp2((s - m) * scale2)
        l = jnp.sum(p, axis=1, keepdims=True)
        o = matmul(p.astype(jnp.bfloat16), tile_of(v_ref, i))

        def step(j, carry):
            m, l, o = carry
            s = matmul_nt(q, tile_of(k_ref, j))
            new = jnp.maximum(m, jnp.max(s, axis=1, keepdims=True))
            p = jnp.exp2((s - new) * scale2)
            fade = jnp.exp2((m - new) * scale2)
            l = l * fade + jnp.sum(p, axis=1, keepdims=True)
            o = o * fade + matmul(p.astype(jnp.bfloat16), tile_of(v_ref, j))
            return new, l, o

        m, l, o = lax.fori_loop(0, i, step, (m, l, o))
        acc[mine, :] = o
        top[mine, :] = jnp.broadcast_to(m, (qtile, HEAD_DIM))
        total[mine, :] = jnp.broadcast_to(l, (qtile, HEAD_DIM))

    @pl.when(member < group - 1)
    def _():
        gather_prefix()

    @pl.loop(0, me)
    def _(u):
        bulk_copy(u, u).wait_recv()
        for s in range(CAP):
            states[u * CAP + s] = matmul_tn(
                feature(recv[u * CAP + s, 0].astype(jnp.float32)).astype(jnp.bfloat16),
                recv[u * CAP + s, 1],
            )

    @pl.when(me == 0)
    def _():
        att[...] = acc[...] / total[...]
        lin[...] = jnp.zeros_like(lin)

    @pl.when(me > 0)
    def _():
        @pl.loop(0, rows // qtile)
        def _(i):
            mine = pl.ds(pl.multiple_of(i * qtile, qtile), qtile)
            q = q_ref[mine, :]
            qf = feature(q.astype(jnp.float32)).astype(jnp.bfloat16)
            qf = jnp.concatenate([qf, qf], axis=1)
            scores, values, linear = [], [], []
            for b in range(per_tile):
                inside = slice(b * BLOCK, (b + 1) * BLOCK)
                ats = [pos_ref[(i * per_tile + b) * TOPK + c] for c in range(TOPK)]
                keys = jnp.concatenate([recv[at, 0] for at in ats], axis=0)
                scores.append(matmul_nt(q[inside], keys))
                values.append(jnp.concatenate([recv[at, 1] for at in ats], axis=0))
                remaining = entering[...]
                for at in ats:
                    remaining = remaining - states[at]
                coarse = remaining.astype(jnp.bfloat16)
                fine = (remaining - coarse.astype(jnp.float32)).astype(jnp.bfloat16)
                linear.append(matmul(qf[inside], jnp.concatenate([coarse, fine], axis=0)))
            lin[mine, :] = jnp.concatenate(linear, axis=0)
            s = jnp.concatenate(scores, axis=0)
            m_old = top[mine, :][:, :1]
            m = jnp.maximum(m_old, jnp.max(s, axis=1, keepdims=True))
            p = jnp.exp2((s - m) * scale2)
            fade = jnp.exp2((m_old - m) * scale2)
            l = total[mine, :][:, :1] * fade + jnp.sum(p, axis=1, keepdims=True)
            p = p.astype(jnp.bfloat16)
            o = jnp.concatenate(
                [
                    matmul(p[b * BLOCK : (b + 1) * BLOCK], values[b])
                    for b in range(per_tile)
                ],
                axis=0,
            )
            att[mine, :] = (acc[mine, :] * fade + o) / l

    parts = 4
    seg = rows // parts
    sub = lax.broadcasted_iota(jnp.int32, (2 * parts, 2 * HEAD_DIM), 0)

    def pick(i):
        return jnp.where(sub == i, 1.0, 0.0).astype(jnp.bfloat16)

    def halves(x, axis):
        coarse = x.astype(jnp.bfloat16)
        fine = (x - coarse.astype(jnp.float32)).astype(jnp.bfloat16)
        return jnp.concatenate([coarse, fine], axis=axis)

    partial = jnp.zeros((2 * parts, seg), jnp.float32)
    for t in range(parts):
        a = att[t * seg : (t + 1) * seg, :]
        b = lin[t * seg : (t + 1) * seg, :]
        partial = partial + matmul_nt(pick(2 * t), halves(a * a, 1))
        partial = partial + matmul_nt(pick(2 * t + 1), halves(b * b, 1))

    count = 0
    copies = []
    for phase, partners in enumerate(phases):
        sums[phase] = partial
        here = []
        for other in partners:
            copy = pltpu.make_async_remote_copy(
                src_ref=sums.at[phase],
                dst_ref=sums_in.at[count],
                send_sem=sum_send.at[count],
                recv_sem=sum_recv.at[count],
                device_id=(me, other),
                device_id_type=MESH,
            )
            copy.start()
            here.append((copy, count))
            count += 1
        for copy, at in here:
            copy.wait_recv()
            partial = partial + sums_in[at]
        copies += [copy for copy, _ in here]

    scales = lax.rsqrt(partial / (heads * HEAD_DIM) + EPS)
    gain_s, gain_l = gain_s_ref[...], gain_l_ref[...]
    spread = halves(scales, 0)
    lane = lax.broadcasted_iota(jnp.int32, (4 * parts, 2 * HEAD_DIM), 1)
    which = lax.broadcasted_iota(jnp.int32, (4 * parts, 2 * HEAD_DIM), 0) % (2 * parts)
    for t in range(parts):
        span = slice(t * seg, (t + 1) * seg)
        target = jnp.where(lane < HEAD_DIM, 2 * t, 2 * t + 1)
        both = matmul_tn(spread, jnp.where(which == target, 1.0, 0.0).astype(jnp.bfloat16))
        soft, linear = both[:, :HEAD_DIM], both[:, HEAD_DIM:]
        out_ref[span, :] = (
            att[span, :] * soft * gain_s + lin[span, :] * linear * gain_l
        ).astype(jnp.bfloat16)

    for copy in copies:
        copy.wait_send()
    for u in range(views - 1):
        @pl.when(u < me)
        def _():
            plan_copy(me, u).wait_send()
    for w in range(1, views):
        @pl.when(w > me)
        def _():
            bulk_copy(me, w).wait_send()

    for step in range(1, group):
        @pl.when(member + step < group)
        def _():
            member_copy(member, step).wait_send()

    @pl.when((member == group - 1) & (me < views - 1))
    def _():
        for step in range(1, group + 1):
            group_copy(step).wait_send()


def shards(views, heads, splits, q, k, v, lists, gain_s, gain_l):
    rows = q.shape[0]
    per_view = rows // BLOCK
    blocks = views * per_view
    flat = lists.reshape(-1)
    ids = jnp.arange(blocks, dtype=jnp.int32)
    present = jnp.any(flat[:, None] == ids[None, :], axis=0)
    table = present.reshape(views, per_view)
    within = jnp.arange(per_view, dtype=jnp.int32)
    earlier = within[None, :] < within[:, None]
    rank = jnp.sum(table[:, None, :] & earlier[None], axis=2, dtype=jnp.int32)
    slots = jnp.arange(HEAD_DIM, dtype=jnp.int32)
    chosen = table[:, None, :] & (rank[:, None, :] == slots[None, :, None])
    plan = jnp.sum(jnp.where(chosen, within[None, None, :], 0), axis=2, dtype=jnp.int32)
    place = (jnp.arange(views, dtype=jnp.int32)[:, None] * CAP + rank).reshape(-1)
    pos = jnp.sum(jnp.where(flat[:, None] == ids[None, :], place[None, :], 0), axis=1)

    phases = len(splits)
    partners = sum(s - 1 for s in splits)
    f32, bf16 = jnp.float32, jnp.bfloat16
    vmem = pl.BlockSpec(memory_space=pltpu.VMEM)
    hbm = pl.BlockSpec(memory_space=pl.ANY)
    smem = pl.BlockSpec(memory_space=pltpu.SMEM)
    dma = pltpu.SemaphoreType.DMA
    sums = (8, rows // 4)
    return pl.pallas_call(
        functools.partial(kernel, views, heads, splits, rows),
        out_shape=jax.ShapeDtypeStruct(q.shape, bf16),
        in_specs=[hbm, hbm, hbm, vmem, smem, vmem, vmem],
        out_specs=vmem,
        scratch_shapes=[
            pltpu.VMEM((rows, HEAD_DIM), bf16),
            pltpu.VMEM((per_view, BLOCK, HEAD_DIM), bf16),
            pltpu.VMEM((per_view, BLOCK, HEAD_DIM), bf16),
            pltpu.VMEM((views, 1, HEAD_DIM), jnp.int32),
            pltpu.SMEM((views, 1, HEAD_DIM), jnp.int32),
            pltpu.VMEM((views * CAP, 2, BLOCK, HEAD_DIM), bf16),
            pltpu.VMEM((views * CAP, 2, BLOCK, HEAD_DIM), bf16),
            pltpu.VMEM((views * CAP, HEAD_DIM, HEAD_DIM), f32),
            pltpu.VMEM((HEAD_DIM, HEAD_DIM), f32),
            pltpu.VMEM((2, HEAD_DIM, HEAD_DIM), bf16),
            pltpu.VMEM((HEAD_DIM, HEAD_DIM), f32),
            pltpu.VMEM((3, HEAD_DIM, HEAD_DIM), bf16),
            pltpu.VMEM((HEAD_DIM, HEAD_DIM), bf16),
            pltpu.VMEM((rows, HEAD_DIM), f32),
            pltpu.VMEM((rows, HEAD_DIM), f32),
            pltpu.VMEM((rows, HEAD_DIM), f32),
            pltpu.VMEM((rows, HEAD_DIM), f32),
            pltpu.VMEM((rows, HEAD_DIM), f32),
            pltpu.VMEM((phases,) + sums, f32),
            pltpu.VMEM((partners,) + sums, f32),
            dma((views,)),
            dma((views,)),
            dma((views,)),
            dma((views,)),
            dma((4,)),
            dma((4,)),
            dma((4,)),
            dma,
            dma,
            dma((3,)),
            dma((partners,)),
            dma((partners,)),
        ],
        compiler_params=pltpu.CompilerParams(
            collective_id=0, has_side_effects=True, vmem_limit_bytes=48 * 1024 * 1024
        ),
    )(
        q,
        k.reshape(per_view, BLOCK, HEAD_DIM),
        v.reshape(per_view, BLOCK, HEAD_DIM),
        plan.reshape(views, 1, HEAD_DIM),
        pos,
        gain_s[None],
        gain_l[None],
    )


def solution(mesh, splits=SPLITS):
    views, heads = mesh.shape["view"], mesh.shape["head"]
    in_specs = (
        P("view", "head"),
        P("view", "head"),
        P("view", "head"),
        P("view", None),
        P("head"),
        P("head"),
    )
    return jax.shard_map(
        functools.partial(shards, views, heads, splits),
        mesh=mesh,
        in_specs=in_specs,
        out_specs=P("view", "head"),
        check_vma=False,
    )
```

```python
import functools

import jax
import jax.numpy as jnp
from jax import lax
from jax.experimental import pallas as pl
from jax.experimental.pallas import tpu as pltpu
from jax.sharding import PartitionSpec as P

HEAD_DIM = 128
BLOCK = 64
TOPK = 4
CAP = 4
EPS = 1e-06
SPLITS = (8, 4)
MESH = pl.DeviceIdType.MESH
NT = (((1,), (1,)), ((), ()))
TN = (((0,), (0,)), ((), ()))


def feature(x):
    return jnp.where(x > 0, x + 1.0, jnp.exp(jnp.minimum(x, 0.0)))


def matmul(a, b):
    return jnp.dot(a, b, preferred_element_type=jnp.float32)


def matmul_nt(a, b):
    return lax.dot_general(a, b, NT, preferred_element_type=jnp.float32)


def matmul_tn(a, b):
    return lax.dot_general(a, b, TN, preferred_element_type=jnp.float32)


def halves(x, axis):
    coarse = x.astype(jnp.bfloat16)
    fine = (x - coarse.astype(jnp.float32)).astype(jnp.bfloat16)
    return jnp.concatenate([coarse, fine], axis=axis)


def send_order(views):
    half = views // 2
    low, high = list(range(half, views)), []
    while low:
        high.append(low.pop())
        if low:
            high.append(low.pop(0))
    return high + list(range(half - 1, 0, -1))


def listing(views, per_view, lists_ref, plan_ref, place_ref):
    blocks = views * per_view
    ids = lax.broadcasted_iota(jnp.int32, (blocks, per_view), 0)
    ones = [jnp.where(lists_ref[c : c + 1, :] == ids, 1.0, 0.0) for c in range(TOPK)]
    count = matmul(
        sum(ones).astype(jnp.bfloat16), jnp.ones((per_view, HEAD_DIM), jnp.bfloat16)
    )
    present = jnp.where(count > 0.0, 1.0, 0.0)
    down = lax.broadcasted_iota(jnp.int32, (blocks, blocks), 0)
    across = lax.broadcasted_iota(jnp.int32, (blocks, blocks), 1)
    before = (across < down) & (across >= down - down % per_view)
    rank = matmul(jnp.where(before, 1.0, 0.0).astype(jnp.bfloat16), present.astype(jnp.bfloat16))
    ident = lax.broadcasted_iota(jnp.int32, (blocks, HEAD_DIM), 0)
    slot = lax.broadcasted_iota(jnp.int32, (blocks, HEAD_DIM), 1).astype(jnp.float32)
    number = jnp.where(rank == slot, present * (ident % per_view).astype(jnp.float32), 0.0)
    for u in range(views):
        plan_ref[u] = jnp.sum(
            number[u * per_view : (u + 1) * per_view], axis=0, keepdims=True
        ).astype(jnp.int32)
    place = ((ident // per_view * CAP).astype(jnp.float32) + rank)[:, :per_view]
    place_ref[...] = jnp.zeros_like(place_ref)
    for c in range(TOPK):
        place_ref[c : c + 1, :per_view] = jnp.sum(ones[c] * place, axis=0, keepdims=True).astype(jnp.int32)


def kernel(
    views, heads, splits, rows,
    q_hbm, k_hbm, v_hbm, plan_hbm, place_hbm, gain_s_hbm, gain_l_hbm, out_ref,
    q_ref, k_ref, v_ref, gains,
    plan_ref, pos_ref, plans, plan_smem, stage, recv, states, entering, leaving, own_state, members, earlier,
    acc, top, total, att, lin, sums, sums_in,
    plan_send, plan_recv, bulk_send, bulk_recv, member_send, member_recv,
    group_send, group_recv, local_sem, in_sem, sum_send, sum_recv,
):
    me = lax.axis_index("view")
    head = lax.axis_index("head")
    scale2 = 1.4426950408889634 * HEAD_DIM ** (-0.5)
    qtile = min(256, rows)
    group = 4 if views >= 16 else 2

    k_in = pltpu.make_async_copy(k_hbm, k_ref, in_sem.at[0])
    v_in = pltpu.make_async_copy(v_hbm, v_ref, in_sem.at[1])
    q_in = pltpu.make_async_copy(q_hbm, q_ref, in_sem.at[2])
    k_in.start()
    v_in.start()
    q_in.start()
    gain_in = [
        pltpu.make_async_copy(gain_s_hbm, gains.at[0], in_sem.at[3]),
        pltpu.make_async_copy(gain_l_hbm, gains.at[1], in_sem.at[4]),
    ]
    for copy in gain_in:
        copy.start()

    phases = []
    stride = 1
    for size in splits:
        place = head // stride % size
        phases.append([head + ((place + t) % size - place) * stride for t in range(1, size)])
        stride *= size

    plan_in = pltpu.make_async_copy(plan_hbm, plan_ref, local_sem)
    plan_in.start()
    place_in = pltpu.make_async_copy(place_hbm, pos_ref, in_sem.at[5])
    place_in.start()

    barrier = pltpu.get_barrier_semaphore()
    for d in range(1, views):
        pl.semaphore_signal(
            barrier, inc=1, device_id=((me + d) % views, head), device_id_type=MESH
        )
    for partners in phases:
        for other in partners:
            pl.semaphore_signal(barrier, inc=1, device_id=(me, other), device_id_type=MESH)
    pl.semaphore_wait(barrier, views - 1 + sum(len(p) for p in phases))

    plan_in.wait()

    def plan_copy(slot, to):
        return pltpu.make_async_remote_copy(
            src_ref=plan_ref.at[to],
            dst_ref=plans.at[slot],
            send_sem=plan_send.at[to],
            recv_sem=plan_recv.at[slot],
            device_id=(to, head),
            device_id_type=MESH,
        )

    for u in range(views - 1):
        @pl.when(u < me)
        def _():
            plan_copy(me, u).start()

    k_in.wait()
    v_in.wait()
    own_state[...] = matmul_tn(
        feature(k_ref[...].reshape(rows, HEAD_DIM).astype(jnp.float32)).astype(jnp.bfloat16),
        v_ref[...].reshape(rows, HEAD_DIM),
    )
    leaving[0] = own_state[...].astype(jnp.bfloat16)
    member = me % group

    def member_copy(slot, step):
        return pltpu.make_async_remote_copy(
            src_ref=leaving.at[0],
            dst_ref=members.at[slot],
            send_sem=member_send.at[step],
            recv_sem=member_recv.at[slot],
            device_id=((me + step) % views, head),
            device_id_type=MESH,
        )

    for step in range(1, group):
        @pl.when(member + step < group)
        def _():
            member_copy(member, step).start()

    def group_copy(step):
        return pltpu.make_async_remote_copy(
            src_ref=leaving.at[1],
            dst_ref=earlier,
            send_sem=group_send.at[step - 1],
            recv_sem=group_recv,
            device_id=((me + step) % views, head),
            device_id_type=MESH,
        )

    def gather_prefix():
        entering[...] = jnp.zeros_like(entering)
        for slot in range(group - 1):
            @pl.when(slot < member)
            def _():
                member_copy(slot, 1).wait_recv()
                entering[...] += members[slot].astype(jnp.float32)

        @pl.when(me >= group)
        def _():
            group_copy(1).wait_recv()
            entering[...] += earlier[...].astype(jnp.float32)

    for w in range(1, views):
        @pl.when(w > me)
        def _():
            plan_copy(w, w).wait_recv()


    plans_copy = pltpu.make_async_copy(plans, plan_smem, local_sem)
    plans_copy.start()
    plans_copy.wait()

    @pl.when(member == group - 1)
    def _():
        gather_prefix()

        @pl.when(me < views - 1)
        def _():
            leaving[1] = (entering[...] + own_state[...]).astype(jnp.bfloat16)
            for step in range(1, group + 1):
                group_copy(step).start()

    def bulk_copy(slot, to):
        return pltpu.make_async_remote_copy(
            src_ref=stage.at[pl.ds(to * CAP, CAP)],
            dst_ref=recv.at[pl.ds(slot * CAP, CAP)],
            send_sem=bulk_send.at[to],
            recv_sem=bulk_recv.at[slot],
            device_id=(to, head),
            device_id_type=MESH,
        )

    for w in send_order(views):
        @pl.when(w > me)
        def _():
            for s in range(CAP):
                block = plan_smem[w, 0, s]
                stage[w * CAP + s, 0] = k_ref[block]
                stage[w * CAP + s, 1] = v_ref[block]
            bulk_copy(me, w).start()

    row = lax.broadcasted_iota(jnp.int32, (qtile, qtile), 0)
    col = lax.broadcasted_iota(jnp.int32, (qtile, qtile), 1)

    per_tile = qtile // BLOCK

    def tile_of(ref, j):
        return ref[pl.ds(j * per_tile, per_tile)].reshape(qtile, HEAD_DIM)

    q_in.wait()
    place_in.wait()
    for copy in gain_in:
        copy.wait()

    @pl.loop(0, rows // qtile)
    def _(i):
        mine = pl.ds(pl.multiple_of(i * qtile, qtile), qtile)
        q = q_ref[mine, :]
        s = jnp.where(row >= col, matmul_nt(q, tile_of(k_ref, i)), -jnp.inf)
        m = jnp.max(s, axis=1, keepdims=True)
        p = jnp.exp2((s - m) * scale2)
        l = jnp.sum(p, axis=1, keepdims=True)
        o = matmul(p.astype(jnp.bfloat16), tile_of(v_ref, i))

        def step(j, carry):
            m, l, o = carry
            s = matmul_nt(q, tile_of(k_ref, j))
            new = jnp.maximum(m, jnp.max(s, axis=1, keepdims=True))
            p = jnp.exp2((s - new) * scale2)
            fade = jnp.exp2((m - new) * scale2)
            l = l * fade + jnp.sum(p, axis=1, keepdims=True)
            o = o * fade + matmul(p.astype(jnp.bfloat16), tile_of(v_ref, j))
            return new, l, o

        m, l, o = lax.fori_loop(0, i, step, (m, l, o))
        acc[mine, :] = o
        top[mine, :] = jnp.broadcast_to(m, (qtile, HEAD_DIM))
        total[mine, :] = jnp.broadcast_to(l, (qtile, HEAD_DIM))

    @pl.when(member < group - 1)
    def _():
        gather_prefix()

    @pl.loop(0, me)
    def _(u):
        bulk_copy(u, u).wait_recv()
        for s in range(CAP):
            states[u * CAP + s] = matmul_tn(
                feature(recv[u * CAP + s, 0].astype(jnp.float32)).astype(jnp.bfloat16),
                recv[u * CAP + s, 1],
            )

    @pl.when(me == 0)
    def _():
        att[...] = acc[...] / total[...]
        lin[...] = jnp.zeros_like(lin)

    def listed(start):
        mine = slice(start, start + qtile)
        q = q_ref[mine, :]
        qf = feature(q.astype(jnp.float32)).astype(jnp.bfloat16)
        qf = jnp.concatenate([qf, qf], axis=1)
        scores, values, linear = [], [], []
        for b in range(per_tile):
            inside = slice(b * BLOCK, (b + 1) * BLOCK)
            ats = [pos_ref[c, start // BLOCK + b] for c in range(TOPK)]
            keys = jnp.concatenate([recv[at, 0] for at in ats], axis=0)
            scores.append(matmul_nt(q[inside], keys))
            values.append(jnp.concatenate([recv[at, 1] for at in ats], axis=0))
            remaining = entering[...]
            for at in ats:
                remaining = remaining - states[at]
            linear.append(matmul(qf[inside], halves(remaining, 0)))
        s = jnp.concatenate(scores, axis=0)
        m_old = top[mine, :][:, :1]
        m = jnp.maximum(m_old, jnp.max(s, axis=1, keepdims=True))
        p = jnp.exp2((s - m) * scale2)
        fade = jnp.exp2((m_old - m) * scale2)
        l = total[mine, :][:, :1] * fade + jnp.sum(p, axis=1, keepdims=True)
        p = p.astype(jnp.bfloat16)
        o = jnp.concatenate(
            [matmul(p[b * BLOCK : (b + 1) * BLOCK], values[b]) for b in range(per_tile)],
            axis=0,
        )
        return (acc[mine, :] * fade + o) / l, jnp.concatenate(linear, axis=0)

    parts = 4
    seg = rows // parts
    chunk = min(seg, HEAD_DIM)
    chunks = seg // chunk
    height = 2 * chunks
    sub = lax.broadcasted_iota(jnp.int32, (height, 2 * HEAD_DIM), 0)

    def pick(i):
        return jnp.where(sub == i, 1.0, 0.0).astype(jnp.bfloat16)

    def squares(t):
        partial = jnp.zeros((height, chunk), jnp.float32)
        for c in range(chunks):
            span = slice(t * seg + c * chunk, t * seg + (c + 1) * chunk)
            a, b = att[span, :], lin[span, :]
            partial = partial + matmul_nt(pick(2 * c), halves(a * a, 1))
            partial = partial + matmul_nt(pick(2 * c + 1), halves(b * b, 1))
        return partial

    sent = []
    waiting = {}

    def exchange(t, phase, partial):
        sums[t, phase] = partial
        base = sum(len(p) for p in phases[:phase])
        waiting[t, phase] = []
        for n, other in enumerate(phases[phase]):
            copy = pltpu.make_async_remote_copy(
                src_ref=sums.at[t, phase],
                dst_ref=sums_in.at[t, base + n],
                send_sem=sum_send.at[t, base + n],
                recv_sem=sum_recv.at[t, base + n],
                device_id=(me, other),
                device_id_type=MESH,
            )
            copy.start()
            waiting[t, phase].append((copy, base + n))
            sent.append(copy)

    def collect(t, phase):
        partial = sums[t, phase]
        for copy, at in waiting[t, phase]:
            copy.wait_recv()
            partial = partial + sums_in[t, at]
        return partial

    def finish(t):
        spread = halves(lax.rsqrt(collect(t, 1) / (heads * HEAD_DIM) + EPS), 0)
        lane = lax.broadcasted_iota(jnp.int32, (2 * height, 2 * HEAD_DIM), 1)
        which = lax.broadcasted_iota(jnp.int32, (2 * height, 2 * HEAD_DIM), 0) % height
        for c in range(chunks):
            span = slice(t * seg + c * chunk, t * seg + (c + 1) * chunk)
            target = jnp.where(lane < HEAD_DIM, 2 * c, 2 * c + 1)
            both = matmul_tn(spread, jnp.where(which == target, 1.0, 0.0).astype(jnp.bfloat16))
            out_ref[span, :] = (
                att[span, :] * both[:, :HEAD_DIM] * gains[0]
                + lin[span, :] * both[:, HEAD_DIM:] * gains[1]
            ).astype(jnp.bfloat16)

    for t in range(parts):
        @pl.when(me > 0)
        def _():
            for start in range(t * seg, (t + 1) * seg, qtile):
                attended, linear = listed(start)
                att[start : start + qtile, :] = attended
                lin[start : start + qtile, :] = linear

        exchange(t, 0, squares(t))
        if t > 0:
            exchange(t - 1, 1, collect(t - 1, 0))
    finish(0)
    exchange(parts - 1, 1, collect(parts - 1, 0))
    for t in range(1, parts):
        finish(t)

    for copy in sent:
        copy.wait_send()
    for u in range(views - 1):
        @pl.when(u < me)
        def _():
            plan_copy(me, u).wait_send()
    for w in range(1, views):
        @pl.when(w > me)
        def _():
            bulk_copy(me, w).wait_send()

    for step in range(1, group):
        @pl.when(member + step < group)
        def _():
            member_copy(member, step).wait_send()

    @pl.when((member == group - 1) & (me < views - 1))
    def _():
        for step in range(1, group + 1):
            group_copy(step).wait_send()


def shards(views, heads, splits, q, k, v, lists, gain_s, gain_l):
    rows = q.shape[0]
    per_view = rows // BLOCK
    plan, place = pl.pallas_call(
        functools.partial(listing, views, per_view),
        out_shape=(
            jax.ShapeDtypeStruct((views, 1, HEAD_DIM), jnp.int32),
            jax.ShapeDtypeStruct((TOPK, HEAD_DIM), jnp.int32),
        ),
        in_specs=[pl.BlockSpec(memory_space=pltpu.VMEM)],
        out_specs=(pl.BlockSpec(memory_space=pltpu.VMEM),) * 2,
    )(lists.T)

    phases = len(splits)
    partners = sum(s - 1 for s in splits)
    f32, bf16 = jnp.float32, jnp.bfloat16
    vmem = pl.BlockSpec(memory_space=pltpu.VMEM)
    hbm = pl.BlockSpec(memory_space=pltpu.HBM)
    dma = pltpu.SemaphoreType.DMA
    parts = 4
    chunk = min(rows // parts, HEAD_DIM)
    sums = (2 * (rows // parts // chunk), chunk)
    return pl.pallas_call(
        functools.partial(kernel, views, heads, splits, rows),
        out_shape=jax.ShapeDtypeStruct(q.shape, bf16),
        in_specs=[hbm] * 7,
        out_specs=vmem,
        scratch_shapes=[
            pltpu.VMEM((rows, HEAD_DIM), bf16),
            pltpu.VMEM((per_view, BLOCK, HEAD_DIM), bf16),
            pltpu.VMEM((per_view, BLOCK, HEAD_DIM), bf16),
            pltpu.VMEM((2, 1, HEAD_DIM), f32),
            pltpu.VMEM((views, 1, HEAD_DIM), jnp.int32),
            pltpu.SMEM((TOPK, HEAD_DIM), jnp.int32),
            pltpu.VMEM((views, 1, HEAD_DIM), jnp.int32),
            pltpu.SMEM((views, 1, HEAD_DIM), jnp.int32),
            pltpu.VMEM((views * CAP, 2, BLOCK, HEAD_DIM), bf16),
            pltpu.VMEM((views * CAP, 2, BLOCK, HEAD_DIM), bf16),
            pltpu.VMEM((views * CAP, HEAD_DIM, HEAD_DIM), f32),
            pltpu.VMEM((HEAD_DIM, HEAD_DIM), f32),
            pltpu.VMEM((2, HEAD_DIM, HEAD_DIM), bf16),
            pltpu.VMEM((HEAD_DIM, HEAD_DIM), f32),
            pltpu.VMEM((3, HEAD_DIM, HEAD_DIM), bf16),
            pltpu.VMEM((HEAD_DIM, HEAD_DIM), bf16),
            pltpu.VMEM((rows, HEAD_DIM), f32),
            pltpu.VMEM((rows, HEAD_DIM), f32),
            pltpu.VMEM((rows, HEAD_DIM), f32),
            pltpu.VMEM((rows, HEAD_DIM), f32),
            pltpu.VMEM((rows, HEAD_DIM), f32),
            pltpu.VMEM((parts, phases) + sums, f32),
            pltpu.VMEM((parts, partners) + sums, f32),
            dma((views,)),
            dma((views,)),
            dma((views,)),
            dma((views,)),
            dma((4,)),
            dma((4,)),
            dma((4,)),
            dma,
            dma,
            dma((6,)),
            dma((parts, partners)),
            dma((parts, partners)),
        ],
        compiler_params=pltpu.CompilerParams(
            collective_id=0, has_side_effects=True, vmem_limit_bytes=56 * 1024 * 1024
        ),
    )(
        q,
        k.reshape(per_view, BLOCK, HEAD_DIM),
        v.reshape(per_view, BLOCK, HEAD_DIM),
        plan,
        place,
        gain_s[None],
        gain_l[None],
    )


def solution(mesh, splits=SPLITS):
    views, heads = mesh.shape["view"], mesh.shape["head"]
    in_specs = (
        P("view", "head"),
        P("view", "head"),
        P("view", "head"),
        P("view", None),
        P("head"),
        P("head"),
    )
    return jax.shard_map(
        functools.partial(shards, views, heads, splits),
        mesh=mesh,
        in_specs=in_specs,
        out_specs=P("view", "head"),
        check_vma=False,
    )
```

```python
import functools

import jax
import jax.numpy as jnp
from jax import lax
from jax.experimental import pallas as pl
from jax.experimental.pallas import tpu as pltpu
from jax.sharding import PartitionSpec as P

HEAD_DIM = 128
BLOCK = 64
TOPK = 4
CAP = 4
EPS = 1e-06
SPLITS = (8, 4)
MESH = pl.DeviceIdType.MESH
NT = (((1,), (1,)), ((), ()))
TN = (((0,), (0,)), ((), ()))


def feature(x):
    return jnp.where(x > 0, x + 1.0, jnp.exp(jnp.minimum(x, 0.0)))


def matmul(a, b):
    return jnp.dot(a, b, preferred_element_type=jnp.float32)


def matmul_nt(a, b):
    return lax.dot_general(a, b, NT, preferred_element_type=jnp.float32)


def matmul_tn(a, b):
    return lax.dot_general(a, b, TN, preferred_element_type=jnp.float32)


def halves(x, axis):
    coarse = x.astype(jnp.bfloat16)
    fine = (x - coarse.astype(jnp.float32)).astype(jnp.bfloat16)
    return jnp.concatenate([coarse, fine], axis=axis)


def send_order(views):
    half = views // 2
    low, high = list(range(half, views)), []
    while low:
        high.append(low.pop())
        if low:
            high.append(low.pop(0))
    return high + list(range(half - 1, 0, -1))


def kernel(
    views, heads, splits, rows,
    q_hbm, k_hbm, v_hbm, lists_hbm, gain_s_hbm, gain_l_hbm, out_ref,
    q_ref, k_ref, v_ref, gains,
    lists_ref, plan_ref, place_ref, pos_ref, plans, plan_smem, stage, recv, states, entering, leaving, own_state, members, earlier,
    acc, top, total, att, lin, sums, sums_in,
    plan_send, plan_recv, bulk_send, bulk_recv, member_send, member_recv,
    group_send, group_recv, local_sem, in_sem, sum_send, sum_recv,
):
    me = lax.axis_index("view")
    head = lax.axis_index("head")
    scale2 = 1.4426950408889634 * HEAD_DIM ** (-0.5)
    qtile = min(256, rows)
    group = 4 if views >= 16 else 2

    k_in = pltpu.make_async_copy(k_hbm, k_ref, in_sem.at[0])
    v_in = pltpu.make_async_copy(v_hbm, v_ref, in_sem.at[1])
    q_in = pltpu.make_async_copy(q_hbm, q_ref, in_sem.at[2])
    k_in.start()
    v_in.start()
    q_in.start()
    gain_in = [
        pltpu.make_async_copy(gain_s_hbm, gains.at[0], in_sem.at[3]),
        pltpu.make_async_copy(gain_l_hbm, gains.at[1], in_sem.at[4]),
    ]
    for copy in gain_in:
        copy.start()

    phases = []
    stride = 1
    for size in splits:
        place = head // stride % size
        phases.append([head + ((place + t) % size - place) * stride for t in range(1, size)])
        stride *= size

    lists_in = pltpu.make_async_copy(lists_hbm, lists_ref, local_sem)
    lists_in.start()

    barrier = pltpu.get_barrier_semaphore()
    for d in range(1, views):
        pl.semaphore_signal(
            barrier, inc=1, device_id=((me + d) % views, head), device_id_type=MESH
        )
    for partners in phases:
        for other in partners:
            pl.semaphore_signal(barrier, inc=1, device_id=(me, other), device_id_type=MESH)
    lists_in.wait()
    per_view = rows // BLOCK
    blocks = views * per_view
    ids = lax.broadcasted_iota(jnp.int32, (blocks, per_view), 0)
    ones = [jnp.where(lists_ref[c : c + 1, :] == ids, 1.0, 0.0) for c in range(TOPK)]
    count = matmul(
        sum(ones).astype(jnp.bfloat16), jnp.ones((per_view, HEAD_DIM), jnp.bfloat16)
    )
    present = jnp.where(count > 0.0, 1.0, 0.0)
    down = lax.broadcasted_iota(jnp.int32, (blocks, blocks), 0)
    across = lax.broadcasted_iota(jnp.int32, (blocks, blocks), 1)
    before = (across < down) & (across >= down - down % per_view)
    rank = matmul(jnp.where(before, 1.0, 0.0).astype(jnp.bfloat16), present.astype(jnp.bfloat16))
    ident = lax.broadcasted_iota(jnp.int32, (blocks, HEAD_DIM), 0)
    slot = lax.broadcasted_iota(jnp.int32, (blocks, HEAD_DIM), 1).astype(jnp.float32)
    number = jnp.where(rank == slot, present * (ident % per_view).astype(jnp.float32), 0.0)
    for u in range(views):
        listed_here = jnp.sum(number[u * per_view : (u + 1) * per_view], axis=0, keepdims=True)
        plan_ref[u] = jnp.clip(listed_here.astype(jnp.int32), 0, per_view - 1)
    place = ((ident // per_view * CAP).astype(jnp.float32) + rank)[:, :per_view]
    place_ref[...] = jnp.zeros_like(place_ref)
    for c in range(TOPK):
        entry = jnp.sum(ones[c] * place, axis=0, keepdims=True).astype(jnp.int32)
        place_ref[c : c + 1, :per_view] = jnp.clip(entry, 0, views * CAP - 1)
    place_in = pltpu.make_async_copy(place_ref, pos_ref, in_sem.at[5])
    place_in.start()

    pl.semaphore_wait(barrier, views - 1 + sum(len(p) for p in phases))

    def plan_copy(slot, to):
        return pltpu.make_async_remote_copy(
            src_ref=plan_ref.at[to],
            dst_ref=plans.at[slot],
            send_sem=plan_send.at[to],
            recv_sem=plan_recv.at[slot],
            device_id=(to, head),
            device_id_type=MESH,
        )

    for u in range(views - 1):
        @pl.when(u < me)
        def _():
            plan_copy(me, u).start()

    k_in.wait()
    v_in.wait()
    own_state[...] = matmul_tn(
        feature(k_ref[...].reshape(rows, HEAD_DIM).astype(jnp.float32)).astype(jnp.bfloat16),
        v_ref[...].reshape(rows, HEAD_DIM),
    )
    leaving[0] = own_state[...].astype(jnp.bfloat16)
    member = me % group

    def member_copy(slot, step):
        return pltpu.make_async_remote_copy(
            src_ref=leaving.at[0],
            dst_ref=members.at[slot],
            send_sem=member_send.at[step],
            recv_sem=member_recv.at[slot],
            device_id=((me + step) % views, head),
            device_id_type=MESH,
        )

    for step in range(1, group):
        @pl.when(member + step < group)
        def _():
            member_copy(member, step).start()

    def group_copy(step, source):
        return pltpu.make_async_remote_copy(
            src_ref=source,
            dst_ref=earlier,
            send_sem=group_send.at[step - 1],
            recv_sem=group_recv,
            device_id=((me + step) % views, head),
            device_id_type=MESH,
        )

    def gather_prefix():
        entering[...] = jnp.zeros_like(entering)
        for slot in range(group - 1):
            @pl.when(slot < member)
            def _():
                member_copy(slot, 1).wait_recv()
                entering[...] += members[slot].astype(jnp.float32)

        @pl.when(me >= group)
        def _():
            group_copy(1, earlier).wait_recv()
            entering[...] += earlier[...].astype(jnp.float32)

            @pl.when(member == 0)
            def _():
                for step in range(1, group - 1):
                    group_copy(step, earlier).start()

    for w in range(1, views):
        @pl.when(w > me)
        def _():
            plan_copy(w, w).wait_recv()


    plans_copy = pltpu.make_async_copy(plans, plan_smem, local_sem)
    plans_copy.start()
    plans_copy.wait()

    @pl.when(member == group - 1)
    def _():
        gather_prefix()

        @pl.when(me < views - 1)
        def _():
            leaving[1] = (entering[...] + own_state[...]).astype(jnp.bfloat16)
            for step in (1, group):
                group_copy(step, leaving.at[1]).start()

    def bulk_copy(slot, to):
        return pltpu.make_async_remote_copy(
            src_ref=stage.at[pl.ds(to * CAP, CAP)],
            dst_ref=recv.at[pl.ds(slot * CAP, CAP)],
            send_sem=bulk_send.at[to],
            recv_sem=bulk_recv.at[slot],
            device_id=(to, head),
            device_id_type=MESH,
        )

    for w in send_order(views):
        @pl.when(w > me)
        def _():
            for s in range(CAP):
                block = plan_smem[w, 0, s]
                stage[w * CAP + s, 0] = k_ref[block]
                stage[w * CAP + s, 1] = v_ref[block]
            bulk_copy(me, w).start()

    row = lax.broadcasted_iota(jnp.int32, (qtile, qtile), 0)
    col = lax.broadcasted_iota(jnp.int32, (qtile, qtile), 1)

    per_tile = qtile // BLOCK

    def tile_of(ref, j):
        return ref[pl.ds(j * per_tile, per_tile)].reshape(qtile, HEAD_DIM)

    q_in.wait()
    place_in.wait()
    for copy in gain_in:
        copy.wait()

    @pl.loop(0, rows // qtile)
    def _(i):
        mine = pl.ds(pl.multiple_of(i * qtile, qtile), qtile)
        q = q_ref[mine, :]
        s = jnp.where(row >= col, matmul_nt(q, tile_of(k_ref, i)), -jnp.inf)
        m = jnp.max(s, axis=1, keepdims=True)
        p = jnp.exp2((s - m) * scale2)
        l = jnp.sum(p, axis=1, keepdims=True)
        o = matmul(p.astype(jnp.bfloat16), tile_of(v_ref, i))

        def step(j, carry):
            m, l, o = carry
            s = matmul_nt(q, tile_of(k_ref, j))
            new = jnp.maximum(m, jnp.max(s, axis=1, keepdims=True))
            p = jnp.exp2((s - new) * scale2)
            fade = jnp.exp2((m - new) * scale2)
            l = l * fade + jnp.sum(p, axis=1, keepdims=True)
            o = o * fade + matmul(p.astype(jnp.bfloat16), tile_of(v_ref, j))
            return new, l, o

        m, l, o = lax.fori_loop(0, i, step, (m, l, o))
        acc[mine, :] = o
        top[mine, :] = jnp.broadcast_to(m, (qtile, HEAD_DIM))
        total[mine, :] = jnp.broadcast_to(l, (qtile, HEAD_DIM))

    @pl.when(member < group - 1)
    def _():
        gather_prefix()

    @pl.loop(0, me)
    def _(u):
        bulk_copy(u, u).wait_recv()
        for s in range(CAP):
            states[u * CAP + s] = matmul_tn(
                feature(recv[u * CAP + s, 0].astype(jnp.float32)).astype(jnp.bfloat16),
                recv[u * CAP + s, 1],
            )

    @pl.when(me == 0)
    def _():
        att[...] = acc[...] / total[...]
        lin[...] = jnp.zeros_like(lin)

    def listed(start):
        mine = slice(start, start + qtile)
        q = q_ref[mine, :]
        qf = feature(q.astype(jnp.float32)).astype(jnp.bfloat16)
        qf = jnp.concatenate([qf, qf], axis=1)
        scores, values, linear = [], [], []
        for b in range(per_tile):
            inside = slice(b * BLOCK, (b + 1) * BLOCK)
            ats = [pos_ref[c, start // BLOCK + b] for c in range(TOPK)]
            keys = jnp.concatenate([recv[at, 0] for at in ats], axis=0)
            scores.append(matmul_nt(q[inside], keys))
            values.append(jnp.concatenate([recv[at, 1] for at in ats], axis=0))
            remaining = entering[...]
            for at in ats:
                remaining = remaining - states[at]
            linear.append(matmul(qf[inside], halves(remaining, 0)))
        s = jnp.concatenate(scores, axis=0)
        m_old = top[mine, :][:, :1]
        m = jnp.maximum(m_old, jnp.max(s, axis=1, keepdims=True))
        p = jnp.exp2((s - m) * scale2)
        fade = jnp.exp2((m_old - m) * scale2)
        l = total[mine, :][:, :1] * fade + jnp.sum(p, axis=1, keepdims=True)
        p = p.astype(jnp.bfloat16)
        o = jnp.concatenate(
            [matmul(p[b * BLOCK : (b + 1) * BLOCK], values[b]) for b in range(per_tile)],
            axis=0,
        )
        return (acc[mine, :] * fade + o) / l, jnp.concatenate(linear, axis=0)

    parts = 4
    seg = rows // parts
    chunk = min(seg, HEAD_DIM)
    chunks = seg // chunk
    height = 2 * chunks
    sub = lax.broadcasted_iota(jnp.int32, (height, 2 * HEAD_DIM), 0)

    def pick(i):
        return jnp.where(sub == i, 1.0, 0.0).astype(jnp.bfloat16)

    def squares(t):
        partial = jnp.zeros((height, chunk), jnp.float32)
        for c in range(chunks):
            span = slice(t * seg + c * chunk, t * seg + (c + 1) * chunk)
            a, b = att[span, :], lin[span, :]
            partial = partial + matmul_nt(pick(2 * c), halves(a * a, 1))
            partial = partial + matmul_nt(pick(2 * c + 1), halves(b * b, 1))
        return partial

    sent = []
    waiting = {}

    def exchange(t, phase, partial):
        sums[t, phase] = partial
        base = sum(len(p) for p in phases[:phase])
        waiting[t, phase] = []
        for n, other in enumerate(phases[phase]):
            copy = pltpu.make_async_remote_copy(
                src_ref=sums.at[t, phase],
                dst_ref=sums_in.at[t, base + n],
                send_sem=sum_send.at[t, base + n],
                recv_sem=sum_recv.at[t, base + n],
                device_id=(me, other),
                device_id_type=MESH,
            )
            copy.start()
            waiting[t, phase].append((copy, base + n))
            sent.append(copy)

    def collect(t, phase):
        partial = sums[t, phase]
        for copy, at in waiting[t, phase]:
            copy.wait_recv()
            partial = partial + sums_in[t, at]
        return partial

    def finish(t):
        spread = halves(lax.rsqrt(collect(t, 1) / (heads * HEAD_DIM) + EPS), 0)
        lane = lax.broadcasted_iota(jnp.int32, (2 * height, 2 * HEAD_DIM), 1)
        which = lax.broadcasted_iota(jnp.int32, (2 * height, 2 * HEAD_DIM), 0) % height
        for c in range(chunks):
            span = slice(t * seg + c * chunk, t * seg + (c + 1) * chunk)
            target = jnp.where(lane < HEAD_DIM, 2 * c, 2 * c + 1)
            both = matmul_tn(spread, jnp.where(which == target, 1.0, 0.0).astype(jnp.bfloat16))
            out_ref[span, :] = (
                att[span, :] * both[:, :HEAD_DIM] * gains[0]
                + lin[span, :] * both[:, HEAD_DIM:] * gains[1]
            ).astype(jnp.bfloat16)

    for t in range(parts):
        @pl.when(me > 0)
        def _():
            for start in range(t * seg, (t + 1) * seg, qtile):
                attended, linear = listed(start)
                att[start : start + qtile, :] = attended
                lin[start : start + qtile, :] = linear

        exchange(t, 0, squares(t))
        if t > 0:
            exchange(t - 1, 1, collect(t - 1, 0))
    finish(0)
    exchange(parts - 1, 1, collect(parts - 1, 0))
    for t in range(1, parts):
        finish(t)

    for copy in sent:
        copy.wait_send()
    for u in range(views - 1):
        @pl.when(u < me)
        def _():
            plan_copy(me, u).wait_send()
    for w in range(1, views):
        @pl.when(w > me)
        def _():
            bulk_copy(me, w).wait_send()

    for step in range(1, group):
        @pl.when(member + step < group)
        def _():
            member_copy(member, step).wait_send()

    @pl.when((member == group - 1) & (me < views - 1))
    def _():
        for step in (1, group):
            group_copy(step, leaving.at[1]).wait_send()

    @pl.when((member == 0) & (me >= group))
    def _():
        for step in range(1, group - 1):
            group_copy(step, earlier).wait_send()


def shards(views, heads, splits, q, k, v, lists, gain_s, gain_l):
    rows = q.shape[0]
    per_view = rows // BLOCK
    phases = len(splits)
    partners = sum(s - 1 for s in splits)
    f32, bf16 = jnp.float32, jnp.bfloat16
    vmem = pl.BlockSpec(memory_space=pltpu.VMEM)
    hbm = pl.BlockSpec(memory_space=pltpu.HBM)
    dma = pltpu.SemaphoreType.DMA
    parts = 4
    chunk = min(rows // parts, HEAD_DIM)
    sums = (2 * (rows // parts // chunk), chunk)
    return pl.pallas_call(
        functools.partial(kernel, views, heads, splits, rows),
        out_shape=jax.ShapeDtypeStruct(q.shape, bf16),
        in_specs=[hbm] * 6,
        out_specs=vmem,
        scratch_shapes=[
            pltpu.VMEM((rows, HEAD_DIM), bf16),
            pltpu.VMEM((per_view, BLOCK, HEAD_DIM), bf16),
            pltpu.VMEM((per_view, BLOCK, HEAD_DIM), bf16),
            pltpu.VMEM((2, 1, HEAD_DIM), f32),
            pltpu.VMEM((TOPK, per_view), jnp.int32),
            pltpu.VMEM((views, 1, HEAD_DIM), jnp.int32),
            pltpu.VMEM((TOPK, HEAD_DIM), jnp.int32),
            pltpu.SMEM((TOPK, HEAD_DIM), jnp.int32),
            pltpu.VMEM((views, 1, HEAD_DIM), jnp.int32),
            pltpu.SMEM((views, 1, HEAD_DIM), jnp.int32),
            pltpu.VMEM((views * CAP, 2, BLOCK, HEAD_DIM), bf16),
            pltpu.VMEM((views * CAP, 2, BLOCK, HEAD_DIM), bf16),
            pltpu.VMEM((views * CAP, HEAD_DIM, HEAD_DIM), f32),
            pltpu.VMEM((HEAD_DIM, HEAD_DIM), f32),
            pltpu.VMEM((2, HEAD_DIM, HEAD_DIM), bf16),
            pltpu.VMEM((HEAD_DIM, HEAD_DIM), f32),
            pltpu.VMEM((3, HEAD_DIM, HEAD_DIM), bf16),
            pltpu.VMEM((HEAD_DIM, HEAD_DIM), bf16),
            pltpu.VMEM((rows, HEAD_DIM), f32),
            pltpu.VMEM((rows, HEAD_DIM), f32),
            pltpu.VMEM((rows, HEAD_DIM), f32),
            pltpu.VMEM((rows, HEAD_DIM), f32),
            pltpu.VMEM((rows, HEAD_DIM), f32),
            pltpu.VMEM((parts, phases) + sums, f32),
            pltpu.VMEM((parts, partners) + sums, f32),
            dma((views,)),
            dma((views,)),
            dma((views,)),
            dma((views,)),
            dma((4,)),
            dma((4,)),
            dma((4,)),
            dma,
            dma,
            dma((6,)),
            dma((parts, partners)),
            dma((parts, partners)),
        ],
        compiler_params=pltpu.CompilerParams(
            collective_id=0, has_side_effects=True, vmem_limit_bytes=53 * 1024 * 1024
        ),
    )(
        q,
        k.reshape(per_view, BLOCK, HEAD_DIM),
        v.reshape(per_view, BLOCK, HEAD_DIM),
        lists.T,
        gain_s[None],
        gain_l[None],
    )


def solution(mesh, splits=SPLITS):
    views, heads = mesh.shape["view"], mesh.shape["head"]
    in_specs = (
        P("view", "head"),
        P("view", "head"),
        P("view", "head"),
        P("view", None),
        P("head"),
        P("head"),
    )
    return jax.shard_map(
        functools.partial(shards, views, heads, splits),
        mesh=mesh,
        in_specs=in_specs,
        out_specs=P("view", "head"),
        check_vma=False,
    )
```

```python
import functools

import jax
import jax.numpy as jnp
from jax import lax
from jax.experimental import pallas as pl
from jax.experimental.pallas import tpu as pltpu
from jax.sharding import PartitionSpec as P

HEAD_DIM = 128
BLOCK = 64
TOPK = 4
CAP = 4
EPS = 1e-06
SPLITS = (8, 4)
MESH = pl.DeviceIdType.MESH
NT = (((1,), (1,)), ((), ()))
TN = (((0,), (0,)), ((), ()))


def feature(x):
    return jnp.where(x > 0, x + 1.0, jnp.exp(jnp.minimum(x, 0.0)))


def matmul(a, b):
    return jnp.dot(a, b, preferred_element_type=jnp.float32)


def matmul_nt(a, b):
    return lax.dot_general(a, b, NT, preferred_element_type=jnp.float32)


def matmul_tn(a, b):
    return lax.dot_general(a, b, TN, preferred_element_type=jnp.float32)


def halves(x, axis):
    coarse = x.astype(jnp.bfloat16)
    fine = (x - coarse.astype(jnp.float32)).astype(jnp.bfloat16)
    return jnp.concatenate([coarse, fine], axis=axis)


def send_order(views):
    half = views // 2
    low, high = list(range(half, views)), []
    while low:
        high.append(low.pop())
        if low:
            high.append(low.pop(0))
    return high + list(range(half - 1, 0, -1))


def kernel(
    views, heads, splits, rows,
    q_hbm, k_hbm, v_hbm, lists_hbm, gain_s_hbm, gain_l_hbm, out_ref,
    q_ref, k_ref, v_ref, gains,
    lists_ref, plan_ref, place_ref, pos_ref, plans, plan_smem, stage, recv, states, entering, leaving, own_state, members, earlier,
    acc, top, total, att, lin, sums, sums_in,
    plan_send, plan_recv, bulk_send, bulk_recv, member_send, member_recv,
    group_send, group_recv, local_sem, in_sem, sum_send, sum_recv,
):
    me = lax.axis_index("view")
    head = lax.axis_index("head")
    scale2 = 1.4426950408889634 * HEAD_DIM ** (-0.5)
    qtile = min(256, rows)
    group = 4 if views >= 16 else 2

    k_in = pltpu.make_async_copy(k_hbm, k_ref, in_sem.at[0])
    v_in = pltpu.make_async_copy(v_hbm, v_ref, in_sem.at[1])
    q_in = pltpu.make_async_copy(q_hbm, q_ref, in_sem.at[2])
    k_in.start()
    v_in.start()
    q_in.start()
    gain_in = [
        pltpu.make_async_copy(gain_s_hbm, gains.at[0], in_sem.at[3]),
        pltpu.make_async_copy(gain_l_hbm, gains.at[1], in_sem.at[4]),
    ]
    for copy in gain_in:
        copy.start()

    phases = []
    stride = 1
    for size in splits:
        place = head // stride % size
        phases.append([head + ((place + t) % size - place) * stride for t in range(1, size)])
        stride *= size

    lists_in = pltpu.make_async_copy(lists_hbm, lists_ref, local_sem)
    lists_in.start()

    barrier = pltpu.get_barrier_semaphore()
    for d in range(1, views):
        pl.semaphore_signal(
            barrier, inc=1, device_id=((me + d) % views, head), device_id_type=MESH
        )
    for partners in phases:
        for other in partners:
            pl.semaphore_signal(barrier, inc=1, device_id=(me, other), device_id_type=MESH)
    lists_in.wait()
    per_view = rows // BLOCK
    blocks = views * per_view
    ids = lax.broadcasted_iota(jnp.int32, (blocks, per_view), 0)
    ones = [jnp.where(lists_ref[c : c + 1, :] == ids, 1.0, 0.0) for c in range(TOPK)]
    count = matmul(
        sum(ones).astype(jnp.bfloat16), jnp.ones((per_view, HEAD_DIM), jnp.bfloat16)
    )
    present = jnp.where(count > 0.0, 1.0, 0.0)
    down = lax.broadcasted_iota(jnp.int32, (blocks, blocks), 0)
    across = lax.broadcasted_iota(jnp.int32, (blocks, blocks), 1)
    before = (across < down) & (across >= down - down % per_view)
    rank = matmul(jnp.where(before, 1.0, 0.0).astype(jnp.bfloat16), present.astype(jnp.bfloat16))
    ident = lax.broadcasted_iota(jnp.int32, (blocks, HEAD_DIM), 0)
    slot = lax.broadcasted_iota(jnp.int32, (blocks, HEAD_DIM), 1).astype(jnp.float32)
    number = jnp.where(rank == slot, present * (ident % per_view).astype(jnp.float32), 0.0)
    for u in range(views):
        listed_here = jnp.sum(number[u * per_view : (u + 1) * per_view], axis=0, keepdims=True)
        plan_ref[u] = jnp.clip(listed_here.astype(jnp.int32), 0, per_view - 1)
    place = ((ident // per_view * CAP).astype(jnp.float32) + rank)[:, :per_view]
    place_ref[...] = jnp.zeros_like(place_ref)
    for c in range(TOPK):
        entry = jnp.sum(ones[c] * place, axis=0, keepdims=True).astype(jnp.int32)
        place_ref[c : c + 1, :per_view] = jnp.clip(entry, 0, views * CAP - 1)
    place_in = pltpu.make_async_copy(place_ref, pos_ref, in_sem.at[5])
    place_in.start()

    pl.semaphore_wait(barrier, views - 1 + sum(len(p) for p in phases))

    def plan_copy(slot, to):
        return pltpu.make_async_remote_copy(
            src_ref=plan_ref.at[to],
            dst_ref=plans.at[slot],
            send_sem=plan_send.at[to],
            recv_sem=plan_recv.at[slot],
            device_id=(to, head),
            device_id_type=MESH,
        )

    for u in range(views - 1):
        @pl.when(u < me)
        def _():
            plan_copy(me, u).start()

    k_in.wait()
    v_in.wait()
    own_state[...] = matmul_tn(
        feature(k_ref[...].reshape(rows, HEAD_DIM).astype(jnp.float32)).astype(jnp.bfloat16),
        v_ref[...].reshape(rows, HEAD_DIM),
    )
    leaving[0] = own_state[...].astype(jnp.bfloat16)
    member = me % group

    def member_copy(slot, step):
        return pltpu.make_async_remote_copy(
            src_ref=leaving.at[0],
            dst_ref=members.at[slot],
            send_sem=member_send.at[step],
            recv_sem=member_recv.at[slot],
            device_id=((me + step) % views, head),
            device_id_type=MESH,
        )

    for step in range(1, group):
        @pl.when(member + step < group)
        def _():
            member_copy(member, step).start()

    def group_copy(step, source):
        return pltpu.make_async_remote_copy(
            src_ref=source,
            dst_ref=earlier,
            send_sem=group_send.at[step - 1],
            recv_sem=group_recv,
            device_id=((me + step) % views, head),
            device_id_type=MESH,
        )

    def gather_prefix():
        entering[...] = jnp.zeros_like(entering)
        for slot in range(group - 1):
            @pl.when(slot < member)
            def _():
                member_copy(slot, 1).wait_recv()
                entering[...] += members[slot].astype(jnp.float32)

        @pl.when(me >= group)
        def _():
            group_copy(1, earlier).wait_recv()
            entering[...] += earlier[...].astype(jnp.float32)

            @pl.when(member == 0)
            def _():
                for step in range(1, group - 1):
                    group_copy(step, earlier).start()

    for w in range(1, views):
        @pl.when(w > me)
        def _():
            plan_copy(w, w).wait_recv()


    plans_copy = pltpu.make_async_copy(plans, plan_smem, local_sem)
    plans_copy.start()
    plans_copy.wait()

    @pl.when(member == group - 1)
    def _():
        gather_prefix()

        @pl.when(me < views - 1)
        def _():
            leaving[1] = (entering[...] + own_state[...]).astype(jnp.bfloat16)
            for step in (1, group):
                group_copy(step, leaving.at[1]).start()

    def bulk_copy(slot, to):
        return pltpu.make_async_remote_copy(
            src_ref=stage.at[pl.ds(to * CAP, CAP)],
            dst_ref=recv.at[pl.ds(slot * CAP, CAP)],
            send_sem=bulk_send.at[to],
            recv_sem=bulk_recv.at[slot],
            device_id=(to, head),
            device_id_type=MESH,
        )

    half = views // 2

    def send_blocks(w, when):
        @pl.when(when)
        def _():
            for s in range(CAP):
                block = plan_smem[w, 0, s]
                stage[w * CAP + s, 0] = k_ref[block]
                stage[w * CAP + s, 1] = v_ref[block]
            bulk_copy(me, w).start()

    def first(w):
        return half < w < half + 7

    for w in send_order(views):
        send_blocks(w, (w > me) & ((me >= half) | first(w)))

    row = lax.broadcasted_iota(jnp.int32, (qtile, qtile), 0)
    col = lax.broadcasted_iota(jnp.int32, (qtile, qtile), 1)

    per_tile = qtile // BLOCK

    def tile_of(ref, j):
        return ref[pl.ds(j * per_tile, per_tile)].reshape(qtile, HEAD_DIM)

    q_in.wait()
    place_in.wait()
    for copy in gain_in:
        copy.wait()

    @pl.loop(0, rows // qtile)
    def _(i):
        mine = pl.ds(pl.multiple_of(i * qtile, qtile), qtile)
        q = q_ref[mine, :]
        s = jnp.where(row >= col, matmul_nt(q, tile_of(k_ref, i)), -jnp.inf)
        m = jnp.max(s, axis=1, keepdims=True)
        p = jnp.exp2((s - m) * scale2)
        l = jnp.sum(p, axis=1, keepdims=True)
        o = matmul(p.astype(jnp.bfloat16), tile_of(v_ref, i))

        def step(j, carry):
            m, l, o = carry
            s = matmul_nt(q, tile_of(k_ref, j))
            new = jnp.maximum(m, jnp.max(s, axis=1, keepdims=True))
            p = jnp.exp2((s - new) * scale2)
            fade = jnp.exp2((m - new) * scale2)
            l = l * fade + jnp.sum(p, axis=1, keepdims=True)
            o = o * fade + matmul(p.astype(jnp.bfloat16), tile_of(v_ref, j))
            return new, l, o

        m, l, o = lax.fori_loop(0, i, step, (m, l, o))
        acc[mine, :] = o
        top[mine, :] = jnp.broadcast_to(m, (qtile, HEAD_DIM))
        total[mine, :] = jnp.broadcast_to(l, (qtile, HEAD_DIM))

    for w in send_order(views):
        if not first(w):
            send_blocks(w, (w > me) & (me < half))

    @pl.when(member < group - 1)
    def _():
        gather_prefix()

    @pl.loop(0, me)
    def _(u):
        bulk_copy(u, u).wait_recv()
        for s in range(CAP):
            states[u * CAP + s] = matmul_tn(
                feature(recv[u * CAP + s, 0].astype(jnp.float32)).astype(jnp.bfloat16),
                recv[u * CAP + s, 1],
            )

    @pl.when(me == 0)
    def _():
        att[...] = acc[...] / total[...]
        lin[...] = jnp.zeros_like(lin)

    def listed(start):
        mine = slice(start, start + qtile)
        q = q_ref[mine, :]
        qf = feature(q.astype(jnp.float32)).astype(jnp.bfloat16)
        qf = jnp.concatenate([qf, qf], axis=1)
        scores, values, linear = [], [], []
        for b in range(per_tile):
            inside = slice(b * BLOCK, (b + 1) * BLOCK)
            ats = [pos_ref[c, start // BLOCK + b] for c in range(TOPK)]
            keys = jnp.concatenate([recv[at, 0] for at in ats], axis=0)
            scores.append(matmul_nt(q[inside], keys))
            values.append(jnp.concatenate([recv[at, 1] for at in ats], axis=0))
            remaining = entering[...]
            for at in ats:
                remaining = remaining - states[at]
            linear.append(matmul(qf[inside], halves(remaining, 0)))
        s = jnp.concatenate(scores, axis=0)
        m_old = top[mine, :][:, :1]
        m = jnp.maximum(m_old, jnp.max(s, axis=1, keepdims=True))
        p = jnp.exp2((s - m) * scale2)
        fade = jnp.exp2((m_old - m) * scale2)
        l = total[mine, :][:, :1] * fade + jnp.sum(p, axis=1, keepdims=True)
        p = p.astype(jnp.bfloat16)
        o = jnp.concatenate(
            [matmul(p[b * BLOCK : (b + 1) * BLOCK], values[b]) for b in range(per_tile)],
            axis=0,
        )
        return (acc[mine, :] * fade + o) / l, jnp.concatenate(linear, axis=0)

    parts = 4
    seg = rows // parts
    chunk = min(seg, HEAD_DIM)
    chunks = seg // chunk
    height = 2 * chunks
    sub = lax.broadcasted_iota(jnp.int32, (height, 2 * HEAD_DIM), 0)

    def pick(i):
        return jnp.where(sub == i, 1.0, 0.0).astype(jnp.bfloat16)

    def squares(t):
        partial = jnp.zeros((height, chunk), jnp.float32)
        for c in range(chunks):
            span = slice(t * seg + c * chunk, t * seg + (c + 1) * chunk)
            a, b = att[span, :], lin[span, :]
            partial = partial + matmul_nt(pick(2 * c), halves(a * a, 1))
            partial = partial + matmul_nt(pick(2 * c + 1), halves(b * b, 1))
        return partial

    sent = []
    waiting = {}

    def exchange(t, phase, partial):
        sums[t, phase] = partial
        base = sum(len(p) for p in phases[:phase])
        waiting[t, phase] = []
        for n, other in enumerate(phases[phase]):
            copy = pltpu.make_async_remote_copy(
                src_ref=sums.at[t, phase],
                dst_ref=sums_in.at[t, base + n],
                send_sem=sum_send.at[t, base + n],
                recv_sem=sum_recv.at[t, base + n],
                device_id=(me, other),
                device_id_type=MESH,
            )
            copy.start()
            waiting[t, phase].append((copy, base + n))
            sent.append(copy)

    def collect(t, phase):
        partial = sums[t, phase]
        for copy, at in waiting[t, phase]:
            copy.wait_recv()
            partial = partial + sums_in[t, at]
        return partial

    def finish(t):
        spread = halves(lax.rsqrt(collect(t, 1) / (heads * HEAD_DIM) + EPS), 0)
        lane = lax.broadcasted_iota(jnp.int32, (2 * height, 2 * HEAD_DIM), 1)
        which = lax.broadcasted_iota(jnp.int32, (2 * height, 2 * HEAD_DIM), 0) % height
        for c in range(chunks):
            span = slice(t * seg + c * chunk, t * seg + (c + 1) * chunk)
            target = jnp.where(lane < HEAD_DIM, 2 * c, 2 * c + 1)
            both = matmul_tn(spread, jnp.where(which == target, 1.0, 0.0).astype(jnp.bfloat16))
            out_ref[span, :] = (
                att[span, :] * both[:, :HEAD_DIM] * gains[0]
                + lin[span, :] * both[:, HEAD_DIM:] * gains[1]
            ).astype(jnp.bfloat16)

    for t in range(parts):
        @pl.when(me > 0)
        def _():
            for start in range(t * seg, (t + 1) * seg, qtile):
                attended, linear = listed(start)
                att[start : start + qtile, :] = attended
                lin[start : start + qtile, :] = linear

        exchange(t, 0, squares(t))
        if t > 0:
            exchange(t - 1, 1, collect(t - 1, 0))
    finish(0)
    exchange(parts - 1, 1, collect(parts - 1, 0))
    for t in range(1, parts):
        finish(t)

    for copy in sent:
        copy.wait_send()
    for u in range(views - 1):
        @pl.when(u < me)
        def _():
            plan_copy(me, u).wait_send()
    for w in range(1, views):
        @pl.when(w > me)
        def _():
            bulk_copy(me, w).wait_send()

    for step in range(1, group):
        @pl.when(member + step < group)
        def _():
            member_copy(member, step).wait_send()

    @pl.when((member == group - 1) & (me < views - 1))
    def _():
        for step in (1, group):
            group_copy(step, leaving.at[1]).wait_send()

    @pl.when((member == 0) & (me >= group))
    def _():
        for step in range(1, group - 1):
            group_copy(step, earlier).wait_send()


def shards(views, heads, splits, q, k, v, lists, gain_s, gain_l):
    rows = q.shape[0]
    per_view = rows // BLOCK
    phases = len(splits)
    partners = sum(s - 1 for s in splits)
    f32, bf16 = jnp.float32, jnp.bfloat16
    vmem = pl.BlockSpec(memory_space=pltpu.VMEM)
    hbm = pl.BlockSpec(memory_space=pltpu.HBM)
    dma = pltpu.SemaphoreType.DMA
    parts = 4
    chunk = min(rows // parts, HEAD_DIM)
    sums = (2 * (rows // parts // chunk), chunk)
    return pl.pallas_call(
        functools.partial(kernel, views, heads, splits, rows),
        out_shape=jax.ShapeDtypeStruct(q.shape, bf16),
        in_specs=[hbm] * 6,
        out_specs=vmem,
        scratch_shapes=[
            pltpu.VMEM((rows, HEAD_DIM), bf16),
            pltpu.VMEM((per_view, BLOCK, HEAD_DIM), bf16),
            pltpu.VMEM((per_view, BLOCK, HEAD_DIM), bf16),
            pltpu.VMEM((2, 1, HEAD_DIM), f32),
            pltpu.VMEM((TOPK, per_view), jnp.int32),
            pltpu.VMEM((views, 1, HEAD_DIM), jnp.int32),
            pltpu.VMEM((TOPK, HEAD_DIM), jnp.int32),
            pltpu.SMEM((TOPK, HEAD_DIM), jnp.int32),
            pltpu.VMEM((views, 1, HEAD_DIM), jnp.int32),
            pltpu.SMEM((views, 1, HEAD_DIM), jnp.int32),
            pltpu.VMEM((views * CAP, 2, BLOCK, HEAD_DIM), bf16),
            pltpu.VMEM((views * CAP, 2, BLOCK, HEAD_DIM), bf16),
            pltpu.VMEM((views * CAP, HEAD_DIM, HEAD_DIM), f32),
            pltpu.VMEM((HEAD_DIM, HEAD_DIM), f32),
            pltpu.VMEM((2, HEAD_DIM, HEAD_DIM), bf16),
            pltpu.VMEM((HEAD_DIM, HEAD_DIM), f32),
            pltpu.VMEM((3, HEAD_DIM, HEAD_DIM), bf16),
            pltpu.VMEM((HEAD_DIM, HEAD_DIM), bf16),
            pltpu.VMEM((rows, HEAD_DIM), f32),
            pltpu.VMEM((rows, HEAD_DIM), f32),
            pltpu.VMEM((rows, HEAD_DIM), f32),
            pltpu.VMEM((rows, HEAD_DIM), f32),
            pltpu.VMEM((rows, HEAD_DIM), f32),
            pltpu.VMEM((parts, phases) + sums, f32),
            pltpu.VMEM((parts, partners) + sums, f32),
            dma((views,)),
            dma((views,)),
            dma((views,)),
            dma((views,)),
            dma((4,)),
            dma((4,)),
            dma((4,)),
            dma,
            dma,
            dma((6,)),
            dma((parts, partners)),
            dma((parts, partners)),
        ],
        compiler_params=pltpu.CompilerParams(
            collective_id=0, has_side_effects=True, vmem_limit_bytes=53 * 1024 * 1024
        ),
    )(
        q,
        k.reshape(per_view, BLOCK, HEAD_DIM),
        v.reshape(per_view, BLOCK, HEAD_DIM),
        lists.T,
        gain_s[None],
        gain_l[None],
    )


def solution(mesh, splits=SPLITS):
    views, heads = mesh.shape["view"], mesh.shape["head"]
    in_specs = (
        P("view", "head"),
        P("view", "head"),
        P("view", "head"),
        P("view", None),
        P("head"),
        P("head"),
    )
    return jax.shard_map(
        functools.partial(shards, views, heads, splits),
        mesh=mesh,
        in_specs=in_specs,
        out_specs=P("view", "head"),
        check_vma=False,
    )
```

```python
import functools

import jax
import jax.numpy as jnp
from jax import lax
from jax.experimental import pallas as pl
from jax.experimental.pallas import tpu as pltpu
from jax.sharding import PartitionSpec as P

HEAD_DIM = 128
BLOCK = 64
TOPK = 4
CAP = 4
EPS = 1e-06
SPLITS = (8, 4)
MESH = pl.DeviceIdType.MESH
NT = (((1,), (1,)), ((), ()))
TN = (((0,), (0,)), ((), ()))


def feature(x):
    return jnp.where(x > 0, x + 1.0, jnp.exp(jnp.minimum(x, 0.0)))


def matmul(a, b):
    return jnp.dot(a, b, preferred_element_type=jnp.float32)


def matmul_nt(a, b):
    return lax.dot_general(a, b, NT, preferred_element_type=jnp.float32)


def matmul_tn(a, b):
    return lax.dot_general(a, b, TN, preferred_element_type=jnp.float32)


def halves(x, axis):
    coarse = x.astype(jnp.bfloat16)
    fine = (x - coarse.astype(jnp.float32)).astype(jnp.bfloat16)
    return jnp.concatenate([coarse, fine], axis=axis)


def send_order(views):
    half = views // 2
    low, high = list(range(half, views)), []
    while low:
        high.append(low.pop())
        if low:
            high.append(low.pop(0))
    return high + list(range(half - 1, 0, -1))


def kernel(
    views, heads, splits, rows,
    q_hbm, k_hbm, v_hbm, lists_hbm, gain_s_hbm, gain_l_hbm, out_ref,
    q_ref, k_ref, v_ref, gains,
    lists_ref, plan_ref, place_ref, pos_ref, plans, plan_smem, stage, recv, states, entering, leaving, own_state, members, earlier,
    acc, top, total, att, lin, sums, sums_in,
    plan_send, plan_recv, bulk_send, bulk_recv, member_send, member_recv,
    group_send, group_recv, local_sem, in_sem, sum_send, sum_recv,
):
    me = lax.axis_index("view")
    head = lax.axis_index("head")
    scale2 = 1.4426950408889634 * HEAD_DIM ** (-0.5)
    qtile = min(256, rows)
    group = 4 if views >= 16 else 2

    k_in = pltpu.make_async_copy(k_hbm, k_ref, in_sem.at[0])
    v_in = pltpu.make_async_copy(v_hbm, v_ref, in_sem.at[1])
    q_in = pltpu.make_async_copy(q_hbm, q_ref, in_sem.at[2])
    k_in.start()
    v_in.start()
    q_in.start()
    gain_in = [
        pltpu.make_async_copy(gain_s_hbm, gains.at[0], in_sem.at[3]),
        pltpu.make_async_copy(gain_l_hbm, gains.at[1], in_sem.at[4]),
    ]
    for copy in gain_in:
        copy.start()

    phases = []
    stride = 1
    for size in splits:
        place = head // stride % size
        phases.append([head + ((place + t) % size - place) * stride for t in range(1, size)])
        stride *= size

    lists_in = pltpu.make_async_copy(lists_hbm, lists_ref, local_sem)
    lists_in.start()

    barrier = pltpu.get_barrier_semaphore()
    for d in range(1, views):
        pl.semaphore_signal(
            barrier, inc=1, device_id=((me + d) % views, head), device_id_type=MESH
        )
    for partners in phases:
        for other in partners:
            pl.semaphore_signal(barrier, inc=1, device_id=(me, other), device_id_type=MESH)
    lists_in.wait()
    per_view = rows // BLOCK
    blocks = views * per_view
    ids = lax.broadcasted_iota(jnp.int32, (blocks, per_view), 0)
    ones = [jnp.where(lists_ref[c : c + 1, :] == ids, 1.0, 0.0) for c in range(TOPK)]
    count = matmul(
        sum(ones).astype(jnp.bfloat16), jnp.ones((per_view, HEAD_DIM), jnp.bfloat16)
    )
    present = jnp.where(count > 0.0, 1.0, 0.0)
    down = lax.broadcasted_iota(jnp.int32, (blocks, blocks), 0)
    across = lax.broadcasted_iota(jnp.int32, (blocks, blocks), 1)
    before = (across < down) & (across >= down - down % per_view)
    rank = matmul(jnp.where(before, 1.0, 0.0).astype(jnp.bfloat16), present.astype(jnp.bfloat16))
    ident = lax.broadcasted_iota(jnp.int32, (blocks, HEAD_DIM), 0)
    slot = lax.broadcasted_iota(jnp.int32, (blocks, HEAD_DIM), 1).astype(jnp.float32)
    number = jnp.where(rank == slot, present * (ident % per_view).astype(jnp.float32), 0.0)
    for u in range(views):
        listed_here = jnp.sum(number[u * per_view : (u + 1) * per_view], axis=0, keepdims=True)
        plan_ref[u] = jnp.clip(listed_here.astype(jnp.int32), 0, per_view - 1)
    place = ((ident // per_view * CAP).astype(jnp.float32) + rank)[:, :per_view]
    place_ref[...] = jnp.zeros_like(place_ref)
    for c in range(TOPK):
        entry = jnp.sum(ones[c] * place, axis=0, keepdims=True).astype(jnp.int32)
        place_ref[c : c + 1, :per_view] = jnp.clip(entry, 0, views * CAP - 1)
    place_in = pltpu.make_async_copy(place_ref, pos_ref, in_sem.at[5])
    place_in.start()

    pl.semaphore_wait(barrier, views - 1 + sum(len(p) for p in phases))

    def plan_copy(slot, to):
        return pltpu.make_async_remote_copy(
            src_ref=plan_ref.at[to],
            dst_ref=plans.at[slot],
            send_sem=plan_send.at[to],
            recv_sem=plan_recv.at[slot],
            device_id=(to, head),
            device_id_type=MESH,
        )

    for u in range(views - 1):
        @pl.when(u < me)
        def _():
            plan_copy(me, u).start()

    k_in.wait()
    v_in.wait()
    own_state[...] = matmul_tn(
        feature(k_ref[...].reshape(rows, HEAD_DIM).astype(jnp.float32)).astype(jnp.bfloat16),
        v_ref[...].reshape(rows, HEAD_DIM),
    )
    leaving[0] = own_state[...].astype(jnp.bfloat16)
    member = me % group

    def member_copy(slot, step):
        return pltpu.make_async_remote_copy(
            src_ref=leaving.at[0],
            dst_ref=members.at[slot],
            send_sem=member_send.at[step],
            recv_sem=member_recv.at[slot],
            device_id=((me + step) % views, head),
            device_id_type=MESH,
        )

    for step in range(1, group):
        @pl.when(member + step < group)
        def _():
            member_copy(member, step).start()

    def group_copy(step, source):
        return pltpu.make_async_remote_copy(
            src_ref=source,
            dst_ref=earlier,
            send_sem=group_send.at[step - 1],
            recv_sem=group_recv,
            device_id=((me + step) % views, head),
            device_id_type=MESH,
        )

    def gather_prefix():
        entering[...] = jnp.zeros_like(entering)
        for slot in range(group - 1):
            @pl.when(slot < member)
            def _():
                member_copy(slot, 1).wait_recv()
                entering[...] += members[slot].astype(jnp.float32)

        @pl.when(me >= group)
        def _():
            group_copy(1, earlier).wait_recv()
            entering[...] += earlier[...].astype(jnp.float32)

            @pl.when(member == 0)
            def _():
                for step in range(1, group - 1):
                    group_copy(step, earlier).start()

    for w in range(1, views):
        @pl.when(w > me)
        def _():
            plan_copy(w, w).wait_recv()


    plans_copy = pltpu.make_async_copy(plans, plan_smem, local_sem)
    plans_copy.start()
    plans_copy.wait()

    @pl.when(member == group - 1)
    def _():
        gather_prefix()

        @pl.when(me < views - 1)
        def _():
            leaving[1] = (entering[...] + own_state[...]).astype(jnp.bfloat16)
            for step in (1, group):
                group_copy(step, leaving.at[1]).start()

    def bulk_copy(slot, to):
        return pltpu.make_async_remote_copy(
            src_ref=stage.at[pl.ds(to * CAP, CAP)],
            dst_ref=recv.at[pl.ds(slot * CAP, CAP)],
            send_sem=bulk_send.at[to],
            recv_sem=bulk_recv.at[slot],
            device_id=(to, head),
            device_id_type=MESH,
        )

    half = views // 2

    def send_blocks(w, when):
        @pl.when(when)
        def _():
            for s in range(CAP):
                block = plan_smem[w, 0, s]
                stage[w * CAP + s, 0] = k_ref[block]
                stage[w * CAP + s, 1] = v_ref[block]
            bulk_copy(me, w).start()

    def first(w):
        return half < w < half + 7

    for w in send_order(views):
        send_blocks(w, (w > me) & ((me >= half) | first(w)))

    row = lax.broadcasted_iota(jnp.int32, (qtile, qtile), 0)
    col = lax.broadcasted_iota(jnp.int32, (qtile, qtile), 1)

    per_tile = qtile // BLOCK

    def tile_of(ref, j):
        return ref[pl.ds(j * per_tile, per_tile)].reshape(qtile, HEAD_DIM)

    q_in.wait()
    place_in.wait()
    for copy in gain_in:
        copy.wait()

    @pl.loop(0, rows // qtile)
    def _(i):
        mine = pl.ds(pl.multiple_of(i * qtile, qtile), qtile)
        q = q_ref[mine, :]
        s = jnp.where(row >= col, matmul_nt(q, tile_of(k_ref, i)), -jnp.inf)
        m = jnp.max(s, axis=1, keepdims=True)
        p = jnp.exp2((s - m) * scale2)
        l = jnp.sum(p, axis=1, keepdims=True)
        o = matmul(p.astype(jnp.bfloat16), tile_of(v_ref, i))

        def step(j, carry):
            m, l, o = carry
            s = matmul_nt(q, tile_of(k_ref, j))
            new = jnp.maximum(m, jnp.max(s, axis=1, keepdims=True))
            p = jnp.exp2((s - new) * scale2)
            fade = jnp.exp2((m - new) * scale2)
            l = l * fade + jnp.sum(p, axis=1, keepdims=True)
            o = o * fade + matmul(p.astype(jnp.bfloat16), tile_of(v_ref, j))
            return new, l, o

        m, l, o = lax.fori_loop(0, i, step, (m, l, o))
        acc[mine, :] = o
        top[mine, :] = jnp.broadcast_to(m, (qtile, HEAD_DIM))
        total[mine, :] = jnp.broadcast_to(l, (qtile, HEAD_DIM))

    for w in send_order(views):
        if not first(w):
            send_blocks(w, (w > me) & (me < half))

    @pl.when(member < group - 1)
    def _():
        gather_prefix()

    @pl.loop(0, me)
    def _(u):
        bulk_copy(u, u).wait_recv()
        for s in range(CAP):
            states[u * CAP + s] = matmul_tn(
                feature(recv[u * CAP + s, 0].astype(jnp.float32)).astype(jnp.bfloat16),
                recv[u * CAP + s, 1],
            )

    @pl.when(me == 0)
    def _():
        att[...] = acc[...] / total[...]
        lin[...] = jnp.zeros_like(lin)

    def listed(start):
        mine = slice(start, start + qtile)
        q = q_ref[mine, :]
        qf = feature(q.astype(jnp.float32)).astype(jnp.bfloat16)
        qf = jnp.concatenate([qf, qf], axis=1)
        scores, values, linear = [], [], []
        for b in range(per_tile):
            inside = slice(b * BLOCK, (b + 1) * BLOCK)
            ats = [pos_ref[c, start // BLOCK + b] for c in range(TOPK)]
            keys = jnp.concatenate([recv[at, 0] for at in ats], axis=0)
            scores.append(matmul_nt(q[inside], keys))
            values.append(jnp.concatenate([recv[at, 1] for at in ats], axis=0))
            remaining = entering[...]
            for at in ats:
                remaining = remaining - states[at]
            linear.append(matmul(qf[inside], halves(remaining, 0)))
        s = jnp.concatenate(scores, axis=0)
        m_old = top[mine, :][:, :1]
        m = jnp.maximum(m_old, jnp.max(s, axis=1, keepdims=True))
        p = jnp.exp2((s - m) * scale2)
        fade = jnp.exp2((m_old - m) * scale2)
        l = total[mine, :][:, :1] * fade + jnp.sum(p, axis=1, keepdims=True)
        p = p.astype(jnp.bfloat16)
        o = jnp.concatenate(
            [matmul(p[b * BLOCK : (b + 1) * BLOCK], values[b]) for b in range(per_tile)],
            axis=0,
        )
        return (acc[mine, :] * fade + o) / l, jnp.concatenate(linear, axis=0)

    parts = 2
    seg = rows // parts
    chunk = min(seg, HEAD_DIM)
    chunks = seg // chunk
    height = 2 * chunks
    sub = lax.broadcasted_iota(jnp.int32, (height, 2 * HEAD_DIM), 0)

    def pick(i):
        return jnp.where(sub == i, 1.0, 0.0).astype(jnp.bfloat16)

    def squares(t):
        partial = jnp.zeros((height, chunk), jnp.float32)
        for c in range(chunks):
            span = slice(t * seg + c * chunk, t * seg + (c + 1) * chunk)
            a, b = att[span, :], lin[span, :]
            partial = partial + matmul_nt(pick(2 * c), halves(a * a, 1))
            partial = partial + matmul_nt(pick(2 * c + 1), halves(b * b, 1))
        return partial

    sent = []
    waiting = {}

    def exchange(t, phase, partial):
        sums[t, phase] = partial
        base = sum(len(p) for p in phases[:phase])
        waiting[t, phase] = []
        for n, other in enumerate(phases[phase]):
            copy = pltpu.make_async_remote_copy(
                src_ref=sums.at[t, phase],
                dst_ref=sums_in.at[t, base + n],
                send_sem=sum_send.at[t, base + n],
                recv_sem=sum_recv.at[t, base + n],
                device_id=(me, other),
                device_id_type=MESH,
            )
            copy.start()
            waiting[t, phase].append((copy, base + n))
            sent.append(copy)

    def collect(t, phase):
        partial = sums[t, phase]
        for copy, at in waiting[t, phase]:
            copy.wait_recv()
            partial = partial + sums_in[t, at]
        return partial

    def finish(t):
        spread = halves(lax.rsqrt(collect(t, 1) / (heads * HEAD_DIM) + EPS), 0)
        lane = lax.broadcasted_iota(jnp.int32, (2 * height, 2 * HEAD_DIM), 1)
        which = lax.broadcasted_iota(jnp.int32, (2 * height, 2 * HEAD_DIM), 0) % height
        for c in range(chunks):
            span = slice(t * seg + c * chunk, t * seg + (c + 1) * chunk)
            target = jnp.where(lane < HEAD_DIM, 2 * c, 2 * c + 1)
            both = matmul_tn(spread, jnp.where(which == target, 1.0, 0.0).astype(jnp.bfloat16))
            out_ref[span, :] = (
                att[span, :] * both[:, :HEAD_DIM] * gains[0]
                + lin[span, :] * both[:, HEAD_DIM:] * gains[1]
            ).astype(jnp.bfloat16)

    for t in range(parts):
        @pl.when(me > 0)
        def _():
            for start in range(t * seg, (t + 1) * seg, qtile):
                attended, linear = listed(start)
                att[start : start + qtile, :] = attended
                lin[start : start + qtile, :] = linear

        exchange(t, 0, squares(t))
        if t > 0:
            exchange(t - 1, 1, collect(t - 1, 0))
    finish(0)
    exchange(parts - 1, 1, collect(parts - 1, 0))
    for t in range(1, parts):
        finish(t)

    for copy in sent:
        copy.wait_send()
    for u in range(views - 1):
        @pl.when(u < me)
        def _():
            plan_copy(me, u).wait_send()
    for w in range(1, views):
        @pl.when(w > me)
        def _():
            bulk_copy(me, w).wait_send()

    for step in range(1, group):
        @pl.when(member + step < group)
        def _():
            member_copy(member, step).wait_send()

    @pl.when((member == group - 1) & (me < views - 1))
    def _():
        for step in (1, group):
            group_copy(step, leaving.at[1]).wait_send()

    @pl.when((member == 0) & (me >= group))
    def _():
        for step in range(1, group - 1):
            group_copy(step, earlier).wait_send()


def shards(views, heads, splits, q, k, v, lists, gain_s, gain_l):
    rows = q.shape[0]
    per_view = rows // BLOCK
    phases = len(splits)
    partners = sum(s - 1 for s in splits)
    f32, bf16 = jnp.float32, jnp.bfloat16
    vmem = pl.BlockSpec(memory_space=pltpu.VMEM)
    hbm = pl.BlockSpec(memory_space=pltpu.HBM)
    dma = pltpu.SemaphoreType.DMA
    parts = 2
    chunk = min(rows // parts, HEAD_DIM)
    sums = (2 * (rows // parts // chunk), chunk)
    return pl.pallas_call(
        functools.partial(kernel, views, heads, splits, rows),
        out_shape=jax.ShapeDtypeStruct(q.shape, bf16),
        in_specs=[hbm] * 6,
        out_specs=vmem,
        scratch_shapes=[
            pltpu.VMEM((rows, HEAD_DIM), bf16),
            pltpu.VMEM((per_view, BLOCK, HEAD_DIM), bf16),
            pltpu.VMEM((per_view, BLOCK, HEAD_DIM), bf16),
            pltpu.VMEM((2, 1, HEAD_DIM), f32),
            pltpu.VMEM((TOPK, per_view), jnp.int32),
            pltpu.VMEM((views, 1, HEAD_DIM), jnp.int32),
            pltpu.VMEM((TOPK, HEAD_DIM), jnp.int32),
            pltpu.SMEM((TOPK, HEAD_DIM), jnp.int32),
            pltpu.VMEM((views, 1, HEAD_DIM), jnp.int32),
            pltpu.SMEM((views, 1, HEAD_DIM), jnp.int32),
            pltpu.VMEM((views * CAP, 2, BLOCK, HEAD_DIM), bf16),
            pltpu.VMEM((views * CAP, 2, BLOCK, HEAD_DIM), bf16),
            pltpu.VMEM((views * CAP, HEAD_DIM, HEAD_DIM), f32),
            pltpu.VMEM((HEAD_DIM, HEAD_DIM), f32),
            pltpu.VMEM((2, HEAD_DIM, HEAD_DIM), bf16),
            pltpu.VMEM((HEAD_DIM, HEAD_DIM), f32),
            pltpu.VMEM((3, HEAD_DIM, HEAD_DIM), bf16),
            pltpu.VMEM((HEAD_DIM, HEAD_DIM), bf16),
            pltpu.VMEM((rows, HEAD_DIM), f32),
            pltpu.VMEM((rows, HEAD_DIM), f32),
            pltpu.VMEM((rows, HEAD_DIM), f32),
            pltpu.VMEM((rows, HEAD_DIM), f32),
            pltpu.VMEM((rows, HEAD_DIM), f32),
            pltpu.VMEM((parts, phases) + sums, f32),
            pltpu.VMEM((parts, partners) + sums, f32),
            dma((views,)),
            dma((views,)),
            dma((views,)),
            dma((views,)),
            dma((4,)),
            dma((4,)),
            dma((4,)),
            dma,
            dma,
            dma((6,)),
            dma((parts, partners)),
            dma((parts, partners)),
        ],
        compiler_params=pltpu.CompilerParams(
            collective_id=0, has_side_effects=True, vmem_limit_bytes=53 * 1024 * 1024
        ),
    )(
        q,
        k.reshape(per_view, BLOCK, HEAD_DIM),
        v.reshape(per_view, BLOCK, HEAD_DIM),
        lists.T,
        gain_s[None],
        gain_l[None],
    )


def solution(mesh, splits=SPLITS):
    views, heads = mesh.shape["view"], mesh.shape["head"]
    in_specs = (
        P("view", "head"),
        P("view", "head"),
        P("view", "head"),
        P("view", None),
        P("head"),
        P("head"),
    )
    return jax.shard_map(
        functools.partial(shards, views, heads, splits),
        mesh=mesh,
        in_specs=in_specs,
        out_specs=P("view", "head"),
        check_vma=False,
    )
```
